32 devices in a mesh: groups: 2 (over y), tile: 4 (over x, core), member: 4 (over z).
Axes of the slice: x: 2, y: 2, z: 4, core: 2. Of those that a mesh axis runs over, the one named last changes fastest.
Arguments:
- fields: bfloat16 [8, 6, 16, 16, 256], P(('groups', 'member'), None, 'tile'), parts along dimension 0, may hold values from -6 to 6
- weight: bfloat16 [2304, 256], P(('tile', 'member')), may hold values from -0.125 to 0.125
- cotangent: bfloat16 [8, 6, 16, 16, 256], P(('groups', 'member'), None, 'tile'), parts along dimension 0, may hold values from -6 to 6
- adjacency: int32 [6, 4, 3], replicated, may hold values from 0 to 5, as said below
Outputs:
- activation: bfloat16 [8, 6, 16, 16, 256], P(('groups', 'member'), None, 'tile'), parts along dimension 0
- input_grad: bfloat16 [8, 6, 16, 16, 256], P(('groups', 'member'), None, 'tile'), parts along dimension 0
- weight_grad: float32 [4608, 256], P(('groups', 'tile', 'member')), parts along dimension 0
The draws below stay inside these ranges and needn't reach their ends.
There are 2 independent parts, one for each index of `groups`. The reference program is written for one: setup_inputs(seed, part) draws one part's arguments, and reference() takes and returns one part's arrays. A program takes and returns all parts, laid end to end along the dimension named above; an argument that names none is the same for every part. Nothing has to cross between parts.
Inputs may be any that keep to these rules, and one draw needn't show every extreme that they name: `adjacency`: each row names a face other than f, an edge 0 to 3 of it and a flag 0 or 1; the pairing is symmetric (edge e of f names edge k of g exactly when edge k of g names edge e of f, with the same flag) and sews the six faces into the surface of a cube.
All inputs are finite; a program needn't handle non-finite values.
Results may differ from the reference program's by a relative error of at most 0.005.
Values may be sent and summed in bfloat16 or wider, within the bound.
A program may use at most 128 MiB of HBM per device.

```python
import math
import jax
import jax.numpy as jnp
import numpy as np
from jax import lax

C = 256
FACE = 16
MEMBERS = 4
KC = 2304
CELLS = 6144


def frame_table():
    normals = np.array([[1, 0, 0], [-1, 0, 0], [0, 1, 0], [0, -1, 0], [0, 0, 1], [0, 0, -1]])
    across = np.array([[0, 1, 0], [0, 1, 0], [0, 0, 1], [0, 0, 1], [1, 0, 0], [1, 0, 0]])
    downward = np.array([[0, 0, 1], [0, 0, -1], [1, 0, 0], [-1, 0, 0], [0, 1, 0], [0, -1, 0]])
    return (normals, across, downward)


def draw_adjacency(key, part):
    normals, across, downward = frame_table()
    order_key, turn_key = jax.random.split(jax.random.fold_in(key, 7))
    order = jax.random.permutation(order_key, 6)
    turns = jax.random.randint(turn_key, (6,), 0, 4)
    normal = jnp.asarray(normals, jnp.int32)[order]
    base_across = jnp.asarray(across, jnp.int32)[order]
    base_down = jnp.asarray(downward, jnp.int32)[order]
    turn_column = turns[:, None]
    axis_across = jnp.where(turn_column == 0, base_across, jnp.where(turn_column == 1, base_down, jnp.where(turn_column == 2, -base_across, -base_down)))
    axis_down = jnp.where(turn_column == 0, base_down, jnp.where(turn_column == 1, -base_across, jnp.where(turn_column == 2, -base_down, base_across)))
    outward = jnp.stack([-axis_down, axis_down, -axis_across, axis_across], axis=1)
    along = jnp.stack([axis_across, axis_across, axis_down, axis_down], axis=1)
    face_ids = jnp.arange(6, dtype=jnp.int32)
    edge_ids = jnp.arange(4, dtype=jnp.int32)
    hits = jnp.all(outward[:, :, None, :] == normal[None, None, :, :], axis=-1)
    neighbour = jnp.sum(hits.astype(jnp.int32) * face_ids, axis=-1)
    backward_hits = jnp.all(outward[neighbour] == normal[:, None, None, :], axis=-1)
    partner_edge = jnp.sum(backward_hits.astype(jnp.int32) * edge_ids, axis=-1)
    partner_along = along[neighbour, partner_edge]
    flipped = (jnp.sum(partner_along * along, axis=-1) < 0).astype(jnp.int32)
    return jnp.stack([neighbour, partner_edge, flipped], axis=-1).astype(jnp.int32)


def block_levels(rng, dims, cuts, smallest, high):
    factor_of, own = 1.0, jax.random.fold_in(rng, 6)
    for axis_at, shards_of in cuts:
        draws = jnp.exp(jax.random.uniform(jax.random.fold_in(own, axis_at), (shards_of,), jnp.float32, smallest / len(cuts), high / len(cuts)))
        factor_of = factor_of * jnp.repeat(draws, dims[axis_at] // shards_of).reshape([-1 if axis == axis_at else 1 for axis in range(len(dims))])
    return factor_of


def centred(own_key, dims, spread, most, cuts=(), held_as=jnp.bfloat16):
    factor_of = block_levels(own_key, dims, cuts, -0.22, 0.18) if cuts else 1.0
    drawn = jax.random.normal(own_key, dims, jnp.float32) * spread * factor_of
    return jnp.minimum(jnp.maximum(drawn, -most), most).astype(held_as)


def setup_inputs(seed: int = 0, part: int = 0) -> dict:
    key_list = jax.random.split(jax.random.key(seed), 5)
    own_keys = jax.random.split(jax.random.fold_in(key_list[4], part), 5)
    fields = centred(own_keys[0], (MEMBERS, 6, FACE, FACE, C), 1.0, 6.0, ((0, 4), (2, 4)))
    weight = centred(key_list[1], (KC, C), KC ** -0.5, 0.125, ((0, 16),))
    cotangent = centred(own_keys[2], (MEMBERS, 6, FACE, FACE, C), 1.0, 6.0, ((0, 4), (2, 4)))
    adjacency = draw_adjacency(jax.random.fold_in(key_list[4], 71), part)
    return {"fields": fields, "weight": weight, "cotangent": cotangent, "adjacency": adjacency}


gelu_scale = 0.7978845608028654

def gelu_tanh(argument):
    return 0.5 * argument * (1.0 + jnp.tanh(gelu_scale * (argument + 0.044715 * argument * argument * argument)))

def boundary_lines(face_fields):
    north_edge = face_fields[:, 0, :, :]
    south_edge = face_fields[:, -1, :, :]
    west_edge = face_fields[:, :, 0, :]
    east_edge = face_fields[:, :, -1, :]
    return jnp.stack([north_edge, south_edge, west_edge, east_edge], axis=1)

def pad_faces(face_fields, adjacency):
    edge_lines = boundary_lines(face_fields)
    picked = edge_lines[adjacency[:, :, 0], adjacency[:, :, 1]]
    flipped = (adjacency[:, :, 2] == 1)[:, :, None, None]
    cycle_cells = jnp.where(flipped, picked[:, :, ::-1, :], picked)
    padded = jnp.pad(face_fields, ((0, 0), (1, 1), (1, 1), (0, 0)))
    padded = padded.at[:, 0, 1:-1].set(cycle_cells[:, 0])
    padded = padded.at[:, -1, 1:-1].set(cycle_cells[:, 1])
    padded = padded.at[:, 1:-1, 0].set(cycle_cells[:, 2])
    padded = padded.at[:, 1:-1, -1].set(cycle_cells[:, 3])
    return padded

def reference(fields, weight, cotangent, adjacency):
    face_size = fields.shape[2]
    channels = fields.shape[4]

    def member_pass(grad_total, inputs):
        face_fields, member_cot = inputs
        padded = pad_faces(face_fields, adjacency)
        pre_act = jnp.zeros((6 * face_size * face_size, channels), jnp.float32)
        for row_step in range(3):
            for col_step in range(3):
                offset = 3 * row_step + col_step
                window = padded[:, row_step:row_step + face_size, col_step:col_step + face_size].reshape(-1, channels)
                pre_act = pre_act + jnp.dot(window, weight[offset * channels:(offset + 1) * channels], preferred_element_type=jnp.float32)
        activation = gelu_tanh(pre_act).astype(jnp.bfloat16)
        unused_value, pullback = jax.vjp(gelu_tanh, pre_act)
        act_grad = pullback(member_cot.reshape(-1, channels).astype(jnp.float32))[0].astype(jnp.bfloat16)
        grad_terms = []
        padded_grad = jnp.zeros((6, face_size + 2, face_size + 2, channels), jnp.float32)
        for row_step in range(3):
            for col_step in range(3):
                offset = 3 * row_step + col_step
                window = padded[:, row_step:row_step + face_size, col_step:col_step + face_size].reshape(-1, channels)
                grad_terms.append(lax.dot_general(window, act_grad, (((0,), (0,)), ((), ())), preferred_element_type=jnp.float32))
                kernel_rows = weight[offset * channels:(offset + 1) * channels]
                product_term = jnp.dot(act_grad, kernel_rows.T, preferred_element_type=jnp.float32).reshape(6, face_size, face_size, channels)
                padded_grad = padded_grad.at[:, row_step:row_step + face_size, col_step:col_step + face_size].add(product_term)
        cycle_grad = jnp.stack([padded_grad[:, 0, 1:-1], padded_grad[:, -1, 1:-1], padded_grad[:, 1:-1, 0], padded_grad[:, 1:-1, -1]], axis=1)
        flipped = (adjacency[:, :, 2] == 1)[:, :, None, None]
        routed = jnp.where(flipped, cycle_grad[:, :, ::-1, :], cycle_grad)
        line_grad = jnp.zeros((6, 4, face_size, channels), jnp.float32).at[adjacency[:, :, 0], adjacency[:, :, 1]].add(routed)
        cell_grad = padded_grad[:, 1:-1, 1:-1]
        cell_grad = cell_grad.at[:, 0, :].add(line_grad[:, 0])
        cell_grad = cell_grad.at[:, -1, :].add(line_grad[:, 1])
        cell_grad = cell_grad.at[:, :, 0].add(line_grad[:, 2])
        cell_grad = cell_grad.at[:, :, -1].add(line_grad[:, 3])
        grad_total = grad_total + jnp.concatenate(grad_terms, axis=0)
        return (grad_total, (activation.reshape(face_fields.shape), cell_grad.astype(jnp.bfloat16)))
    start_grad = jnp.zeros((9 * channels, channels), jnp.float32)
    grad_total, outputs = lax.scan(member_pass, start_grad, (fields, cotangent))
    activation, input_grad = outputs
    weight_grad = grad_total / math.sqrt(CELLS)
    return (activation, input_grad, weight_grad)
```

```python
import functools
import math

import jax
import jax.numpy as jnp
import numpy as np
from jax import lax
from jax.experimental import pallas as pl
from jax.experimental.pallas import tpu as pltpu
from jax.sharding import PartitionSpec as P

gelu_scale = 0.7978845608028654


def from_root(value, axis, source):
    kept = jnp.where(lax.axis_index(axis) == source, value, 0).astype(value.dtype)
    return lax.psum(kept, axis)


def extended(cells, sides, width):
    for axis, dim in sides:
        count = lax.axis_size(axis)
        ends = count - 1
        head = lax.slice_in_dim(cells, 0, width, axis=dim)
        tail = lax.slice_in_dim(cells, cells.shape[dim] - width, cells.shape[dim], axis=dim)
        cells = jnp.concatenate(
            [
                lax.ppermute(tail, axis, [(i, (i + 1) % count) for i in range(ends)]),
                cells,
                lax.ppermute(head, axis, [((i + 1) % count, i) for i in range(ends)]),
            ],
            axis=dim,
        )
    return cells


def gelu_tanh(argument):
    return (
        0.5
        * argument
        * (1.0 + jnp.tanh(gelu_scale * (argument + 0.044715 * argument * argument * argument)))
    )


def edge_selector(adjacency):
    source_index = adjacency[:, :, 2] * 24 + adjacency[:, :, 0] * 4 + adjacency[:, :, 1]
    source_index = source_index.reshape(24)
    return (source_index[:, None] == jnp.arange(48, dtype=jnp.int32)[None, :]).astype(jnp.float32)


def route_lines(cycle_grad, selector):
    members, face_count, edges, face_size, channels = cycle_grad.shape
    flat_cycle = cycle_grad.reshape(members, 24, face_size, channels)
    routed = jnp.einsum("ts,mtfc->msfc", selector, flat_cycle, precision=lax.Precision.HIGHEST)
    line_grad = routed[:, :24] + routed[:, 24:, ::-1]
    return line_grad.reshape(members, face_count, 4, face_size, channels)


def plain_shards(fields, weight, cotangent, adjacency):
    members, face_count, band_rows, face_size, channels = fields.shape
    position = lax.axis_index("tile")
    tile_count = lax.axis_size("tile")
    top_device = position == 0
    bottom_device = position == tile_count - 1
    row_start = position * band_rows
    selector = edge_selector(adjacency)
    full_weight = lax.all_gather(weight, ("tile", "member"), axis=0, tiled=True)
    side_columns = jnp.stack([fields[:, :, :, 0, :], fields[:, :, :, -1, :]], axis=2)
    all_columns = lax.all_gather(side_columns, "tile", axis=3, tiled=True)
    north_lines = from_root(fields[:, :, 0, :, :], "tile", 0)
    south_lines = from_root(fields[:, :, -1, :, :], "tile", tile_count - 1)
    edge_lines = jnp.concatenate(
        [north_lines[:, :, None], south_lines[:, :, None], all_columns], axis=2
    )
    edge_lines = edge_lines.reshape(members, 24, face_size, channels)
    both_ways = jnp.concatenate([edge_lines, edge_lines[:, :, ::-1]], axis=1)
    cycle_cells = jnp.einsum(
        "ts,msfc->mtfc",
        selector.astype(jnp.bfloat16),
        both_ways,
        preferred_element_type=jnp.float32,
    )
    cycle_cells = cycle_cells.astype(jnp.bfloat16).reshape(
        members, face_count, 4, face_size, channels
    )
    side_cycle = lax.dynamic_slice_in_dim(cycle_cells[:, :, 2:4], row_start, band_rows, 3)
    widened = jnp.concatenate(
        [side_cycle[:, :, 0][:, :, :, None], fields, side_cycle[:, :, 1][:, :, :, None]], axis=3
    )
    padded = extended(widened, (("tile", 2),), 1)
    zero_cell = jnp.zeros((members, face_count, 1, channels), jnp.bfloat16)
    north_row = jnp.concatenate([zero_cell, cycle_cells[:, :, 0], zero_cell], axis=2)
    south_row = jnp.concatenate([zero_cell, cycle_cells[:, :, 1], zero_cell], axis=2)
    padded = padded.at[:, :, 0].set(jnp.where(top_device, north_row, padded[:, :, 0]))
    padded = padded.at[:, :, -1].set(jnp.where(bottom_device, south_row, padded[:, :, -1]))
    cell_count = members * face_count * band_rows * face_size
    pre_act = jnp.zeros((cell_count, channels), jnp.float32)
    for row_step in range(3):
        for col_step in range(3):
            offset = 3 * row_step + col_step
            window = padded[
                :, :, row_step : row_step + band_rows, col_step : col_step + face_size
            ].reshape(cell_count, channels)
            pre_act = pre_act + jnp.dot(
                window,
                full_weight[offset * channels : (offset + 1) * channels],
                preferred_element_type=jnp.float32,
            )
    activation = gelu_tanh(pre_act).astype(jnp.bfloat16).reshape(fields.shape)
    unused_value, pullback = jax.vjp(gelu_tanh, pre_act)
    act_grad = pullback(cotangent.reshape(cell_count, channels).astype(jnp.float32))[0].astype(
        jnp.bfloat16
    )
    grad_terms = []
    grad_pad = jnp.zeros((members, face_count, band_rows + 2, face_size + 2, channels), jnp.float32)
    for row_step in range(3):
        for col_step in range(3):
            offset = 3 * row_step + col_step
            window = padded[
                :, :, row_step : row_step + band_rows, col_step : col_step + face_size
            ].reshape(cell_count, channels)
            grad_terms.append(
                lax.dot_general(
                    window, act_grad, (((0,), (0,)), ((), ())), preferred_element_type=jnp.float32
                )
            )
            kernel_rows = full_weight[offset * channels : (offset + 1) * channels]
            product_term = jnp.dot(act_grad, kernel_rows.T, preferred_element_type=jnp.float32)
            product_term = product_term.reshape(members, face_count, band_rows, face_size, channels)
            grad_pad = grad_pad.at[
                :, :, row_step : row_step + band_rows, col_step : col_step + face_size
            ].add(product_term)
    local_grad = jnp.concatenate(grad_terms, axis=0)
    owned_rows = lax.psum_scatter(local_grad, ("tile", "member"), scatter_dimension=0, tiled=True)
    total_cells = cell_count * tile_count * lax.axis_size("member")
    weight_grad = owned_rows / math.sqrt(total_cells)
    cycle_rows = jnp.stack([grad_pad[:, :, 0], grad_pad[:, :, -1]], axis=2)
    received = extended(cycle_rows, (("tile", 2),), 1)
    band_grad = grad_pad[:, :, 1:-1]
    band_grad = band_grad.at[:, :, 0].add(received[:, :, 0])
    band_grad = band_grad.at[:, :, -1].add(received[:, :, 3])
    side_grad = jnp.stack([band_grad[:, :, :, 0], band_grad[:, :, :, -1]], axis=2)
    side_full = lax.dynamic_update_slice_in_dim(
        jnp.zeros((members, face_count, 2, face_size, channels), jnp.float32),
        side_grad,
        row_start,
        3,
    )
    north_grad = jnp.where(top_device, grad_pad[:, :, 0, 1:-1], 0.0)
    south_grad = jnp.where(bottom_device, grad_pad[:, :, -1, 1:-1], 0.0)
    cycle_grad = jnp.concatenate(
        [north_grad[:, :, None], south_grad[:, :, None], side_full], axis=2
    )
    line_grad = route_lines(cycle_grad, selector)
    side_share = lax.psum_scatter(
        line_grad[:, :, 2:4].astype(jnp.bfloat16), "tile", scatter_dimension=3, tiled=True
    ).astype(jnp.float32)
    top_bottom = lax.psum(line_grad[:, :, 0:2].astype(jnp.bfloat16), "tile").astype(jnp.float32)
    cell_grad = band_grad[:, :, :, 1:-1]
    cell_grad = cell_grad.at[:, :, :, 0].add(side_share[:, :, 0])
    cell_grad = cell_grad.at[:, :, :, -1].add(side_share[:, :, 1])
    cell_grad = cell_grad.at[:, :, 0].add(jnp.where(top_device, top_bottom[:, :, 0], 0.0))
    cell_grad = cell_grad.at[:, :, -1].add(jnp.where(bottom_device, top_bottom[:, :, 1], 0.0))
    input_grad = cell_grad.astype(jnp.bfloat16)
    return (activation, input_grad, weight_grad)


MESH = pl.DeviceIdType.MESH
COPIES = 30
WZ, WX, WS, WD, EX, GX, R1, X2, Z3 = 0, 3, 7, 11, 15, 18, 21, 23, 27


def one_hot(index_column, width):
    rows = index_column.shape[0]
    lanes = lax.broadcasted_iota(jnp.int32, (rows, width), 1)
    return jnp.where(index_column == lanes, 1.0, 0.0)


def fused_kernel(
    dims,
    scale,
    fields_ref,
    weight_ref,
    cot_ref,
    pad_index_ref,
    cell_index_ref,
    act_ref,
    in_grad_ref,
    w_grad_ref,
    full_w,
    edges,
    grad_edges,
    pick,
    padded,
    shifted,
    total,
    outgoing,
    from_core,
    to_x,
    from_x,
    to_z,
    from_z,
    send_sem,
    recv_sem,
):
    faces, band, size, channels = dims
    cells = faces * band * size
    line = faces * size
    side = faces * 2 * band
    block = weight_ref.shape[0]
    quarter = 4 * block
    f32, bf16 = jnp.float32, jnp.bfloat16
    me = lax.axis_index("tile")
    z = lax.axis_index("member")
    chip, core = me // 2, me % 2
    sib = chip * 2 + (1 - core)
    across = (1 - chip) * 2 + core
    diag = (1 - chip) * 2 + (1 - core)
    tile_peers = (sib, across, diag)

    def remote(src, dst, sem, target):
        return pltpu.make_async_remote_copy(
            src_ref=src,
            dst_ref=dst,
            send_sem=send_sem.at[sem],
            recv_sem=recv_sem.at[sem],
            device_id=target,
            device_id_type=MESH,
        )

    def tile_id(t):
        return {"tile": t}

    def member_id(k):
        return {"member": (z + k) % 4}

    def w_block(t, m):
        return full_w.at[pl.ds(pl.multiple_of((t * 4 + m) * block, 16), block)]

    barrier = pltpu.get_barrier_semaphore()
    for t in tile_peers:
        pl.semaphore_signal(barrier, inc=1, device_id=tile_id(t), device_id_type=MESH)
    for k in range(1, 4):
        pl.semaphore_signal(barrier, inc=1, device_id=member_id(k), device_id_type=MESH)

    side_pick = one_hot(cell_index_ref[0:side, 5:6], cells).astype(bf16)

    def own_edges(values, out):
        cube = values.reshape(faces, band, size, channels)
        out[me, 0:side] = jnp.dot(side_pick, values, preferred_element_type=f32).astype(bf16)
        out[me, side : side + line] = cube[:, 0].reshape(line, channels)
        out[me, side + line : side + 2 * line] = cube[:, band - 1].reshape(line, channels)

    w_block(me, z)[...] = weight_ref[...]
    own_edges(fields_ref[...], edges)
    pl.semaphore_wait(barrier, 6)

    started = []

    def go(copy):
        copy.start()
        started.append(copy)

    for k in (2, 1, 3):
        go(remote(w_block(me, z), w_block(me, z), WZ + k - 1, member_id(k)))
    for k, t in enumerate(tile_peers):
        go(remote(edges.at[me], edges.at[me], EX + k, tile_id(t)))

    def w_spread(k):
        part = w_block(me, (z + 4 - k) % 4)
        if k:
            remote(part, part, WZ + k - 1, member_id(k)).wait_recv()
        go(remote(part, part, WX + k, tile_id(across)))
        go(remote(part, part, WS + k, tile_id(sib)))

    w_spread(0)
    for dx in range(3):
        pick[dx] = one_hot(pad_index_ref[:, dx : dx + 1], 4 * side + 2 * line).astype(bf16)
    for k in (1, 3, 2):
        w_spread(k)

    def columns(rows):
        return lax.broadcasted_iota(jnp.int32, (rows, 1), 0) % size

    def moved(values, step):
        rows = values.shape[0]
        if step == 0:
            return values
        if step < 0:
            return jnp.where(columns(rows) == 0, 0.0, pltpu.roll(values, 1, 0))
        return jnp.where(columns(rows) == size - 1, 0.0, pltpu.roll(values, rows - 1, 0))

    def with_halo(values, buf):
        above = buf[jnp.maximum(me - 1, 0), side + line : side + 2 * line].astype(f32)
        below = buf[jnp.minimum(me + 1, 3), side : side + line].astype(f32)
        above = jnp.where(me > 0, above, 0.0).reshape(faces, 1, size, channels)
        below = jnp.where(me < 3, below, 0.0).reshape(faces, 1, size, channels)
        own = values.astype(f32).reshape(faces, band, size, channels)
        return jnp.concatenate([above, own, below], axis=1).reshape(-1, channels)

    def lines_of(buf):
        return jnp.concatenate(
            [buf[t, 0:side] for t in range(4)]
            + [buf[0, side : side + line], buf[3, side + line : side + 2 * line]],
            axis=0,
        )

    for k, t in enumerate(tile_peers):
        remote(edges.at[t], edges.at[t], EX + k, tile_id(t)).wait_recv()
    lines = lines_of(edges)
    center = with_halo(fields_ref[...], edges)
    for dx in range(3):
        values = moved(center, dx - 1) + jnp.dot(pick[dx], lines, preferred_element_type=f32)
        padded[dx] = values.astype(bf16).reshape(faces, band + 2, size, channels)

    for k in (0, 1, 3, 2):
        part = w_block(across, (z + 4 - k) % 4)
        remote(part, part, WX + k, tile_id(across)).wait_recv()
        go(remote(part, part, WD + k, tile_id(sib)))
    for k in range(4):
        part = w_block(sib, (z + 4 - k) % 4)
        remote(part, part, WS + k, tile_id(sib)).wait_recv()
        part = w_block(diag, (z + 4 - k) % 4)
        remote(part, part, WD + k, tile_id(sib)).wait_recv()

    def window(dy, dx):
        return padded[dx, :, dy : dy + band].reshape(cells, channels)

    def w_of(dy, dx):
        first = (3 * dy + dx) * channels
        return full_w[first : first + channels]

    pre = jnp.zeros((cells, channels), f32)
    for dy in range(3):
        for dx in range(3):
            pre = pre + jnp.dot(window(dy, dx), w_of(dy, dx), preferred_element_type=f32)
    square = pre * pre
    bend = jnp.tanh(gelu_scale * (pre + 0.044715 * pre * square))
    act_ref[...] = (0.5 * pre * (1.0 + bend)).astype(bf16)
    slope = 0.5 * (1.0 + bend) + 0.5 * pre * (1.0 - bend * bend) * (
        gelu_scale * (1.0 + 3 * 0.044715 * square)
    )
    act_grad = (cot_ref[...].astype(f32) * slope).astype(bf16)
    own_edges(act_grad, grad_edges)
    for k, t in enumerate(tile_peers):
        go(remote(grad_edges.at[me], grad_edges.at[me], GX + k, tile_id(t)))

    for dy in range(3):
        for dx in range(3):
            first = (3 * dy + dx) * channels
            part = lax.dot_general(
                window(dy, dx), act_grad, (((0,), (0,)), ((), ())), preferred_element_type=f32
            )
            total[first : first + channels] = part
            outgoing[first : first + channels] = part.astype(bf16)

    def quarter_at(t):
        return pl.ds(pl.multiple_of(t * quarter, 16), quarter)

    def part_at(m):
        return pl.ds(pl.multiple_of(m * block, 16), block)

    def row_at(t, m):
        return pl.ds(pl.multiple_of((t * 4 + m) * block, 16), block)

    go(remote(outgoing.at[quarter_at(diag)], from_core.at[0], R1, tile_id(sib)))
    go(remote(outgoing.at[quarter_at(sib)], from_core.at[1], R1 + 1, tile_id(sib)))

    remote(from_core.at[0], from_core.at[0], R1, tile_id(sib)).wait_recv()
    for k in (2, 1, 3, 0):
        m = (z + k) % 4
        to_x[part_at(m)] = (
            total[row_at(across, m)] + from_core[0, part_at(m)].astype(f32)
        ).astype(bf16)
        go(remote(to_x.at[part_at(m)], from_x.at[part_at(m)], X2 + k, tile_id(across)))

    for k, t in enumerate(tile_peers):
        remote(grad_edges.at[t], grad_edges.at[t], GX + k, tile_id(t)).wait_recv()
    center = with_halo(act_grad, grad_edges)
    for dx in range(3):
        shifted[dx] = (
            moved(center, 1 - dx).astype(bf16).reshape(faces, band + 2, size, channels)
        )
    grad = jnp.zeros((cells, channels), f32)
    over_outputs = (((1,), (1,)), ((), ()))
    for dy in range(3):
        for dx in range(3):
            grad = grad + lax.dot_general(
                shifted[dx, :, 2 - dy : 2 - dy + band].reshape(cells, channels),
                w_of(dy, dx),
                over_outputs,
                preferred_element_type=f32,
            )

    remote(from_core.at[1], from_core.at[1], R1 + 1, tile_id(sib)).wait_recv()
    for k in (2, 1, 3, 0):
        m = (z + k) % 4
        remote(to_x.at[part_at(m)], from_x.at[part_at(m)], X2 + k, tile_id(across)).wait_recv()
        mine = (
            total[row_at(me, m)]
            + from_core[1, part_at(m)].astype(f32)
            + from_x[part_at(m)].astype(f32)
        )
        if k:
            to_z[k - 1] = mine.astype(bf16)
            go(remote(to_z.at[k - 1], from_z.at[k - 1], Z3 + k - 1, member_id(k)))
        else:
            w_grad_ref[...] = mine

    lines = lines_of(grad_edges)
    taps = [
        jnp.dot(
            one_hot(cell_index_ref[:, 2 + s : 3 + s], 4 * side + 2 * line).astype(bf16),
            lines,
            preferred_element_type=f32,
        ).astype(bf16)
        for s in range(3)
    ]
    pieces = []
    for edge in range(4):
        piece = jnp.zeros((line, channels), f32)
        for s in range(3):
            dy, dx = ((0, s), (2, s), (s, 0), (s, 2))[edge]
            piece = piece + lax.dot_general(
                taps[s][edge * line : (edge + 1) * line],
                w_of(dy, dx),
                over_outputs,
                preferred_element_type=f32,
            )
        pieces.append(piece)
    cycle = jnp.concatenate(pieces, axis=0)
    route = (
        one_hot(cell_index_ref[:, 0:1], 4 * line) + one_hot(cell_index_ref[:, 1:2], 4 * line)
    ).astype(bf16)
    high = cycle.astype(bf16)
    low = (cycle - high.astype(f32)).astype(bf16)
    grad = grad + jnp.dot(route, high, preferred_element_type=f32)
    grad = grad + jnp.dot(route, low, preferred_element_type=f32)
    in_grad_ref[...] = grad.astype(bf16)

    result = w_grad_ref[...]
    for k in range(1, 4):
        remote(from_z.at[k - 1], from_z.at[k - 1], Z3 + k - 1, member_id(k)).wait_recv()
        result = result + from_z[k - 1].astype(f32)
    w_grad_ref[...] = result * scale
    for copy in started:
        copy.wait_send()


def index_tables(adjacency, faces, band, size):
    position = lax.axis_index("tile")
    face, edge, flag = (adjacency[:, :, i][:, :, None] for i in range(3))
    along = jnp.arange(size, dtype=jnp.int32)[None, None, :]
    u = jnp.where(flag == 1, size - 1 - along, along)
    side, line = faces * 2 * band, faces * size
    on_rows = 4 * side + edge * line + face * size + u
    on_sides = (u // band) * side + face * 2 * band + (edge - 2) * band + u % band
    source = jnp.where(edge < 2, on_rows, on_sides)
    cycle = edge * line + face * size + u

    def framed(values, inner):
        middle = jnp.full((faces, size, inner), -1, jnp.int32)
        return jnp.concatenate([values[:, 2][:, :, None], middle, values[:, 3][:, :, None]], axis=2)

    def ended(values):
        return jnp.pad(values, ((0, 0), (1, 1)), constant_values=-1)[:, None]

    whole = jnp.concatenate([ended(source[:, 0]), framed(source, size), ended(source[:, 1])], axis=1)
    rows = lax.dynamic_slice_in_dim(whole, position * band, band + 2, 1)
    pad_index = jnp.stack([rows[:, :, dx : dx + size] for dx in range(3)], axis=-1).reshape(-1, 3)
    by_column = framed(cycle, size - 2)
    by_row = jnp.concatenate(
        [
            cycle[:, 0][:, None],
            jnp.full((faces, size - 2, size), -1, jnp.int32),
            cycle[:, 1][:, None],
        ],
        axis=1,
    )
    both = jnp.stack([by_column, by_row], axis=-1)
    both = lax.dynamic_slice_in_dim(both, position * band, band, 1).reshape(-1, 2)

    e, f, t = np.meshgrid(np.arange(4), np.arange(faces), np.arange(size), indexing="ij")
    fixed = np.full((faces * band * size, 4), -1, np.int32)
    for s in range(3):
        v = t + 1 - s
        at = np.where(
            e < 2,
            4 * side + e * line + f * size + v,
            (v // band) * side + f * 2 * band + (e - 2) * band + v % band,
        )
        fixed[:, s] = np.where((v < 0) | (v >= size), -1, at).reshape(-1)
    f, k, r = np.meshgrid(np.arange(faces), np.arange(2), np.arange(band), indexing="ij")
    fixed[:side, 3] = (f * band * size + r * size + k * (size - 1)).reshape(-1)
    cell_index = jnp.concatenate([both, jnp.asarray(fixed)], axis=1)
    return pad_index, cell_index


def shards(fields, weight, cotangent, adjacency):
    members, faces, band, size, channels = fields.shape
    tiles, across = lax.axis_size("tile"), lax.axis_size("member")
    block = weight.shape[0]
    fits = tiles == 4 and across == 4 and members == 1 and band * tiles == size
    if not (fits and size == 16 and block % 16 == 0 and (faces * 2 * band) % 16 == 0):
        return plain_shards(fields, weight, cotangent, adjacency)
    cells = faces * band * size
    pad_index, cell_index = index_tables(adjacency, faces, band, size)
    side, line = faces * 2 * band, faces * size
    bf16, f32 = jnp.bfloat16, jnp.float32
    scale = 1.0 / math.sqrt(cells * tiles * across)
    rows = block * tiles * across
    whole = pl.BlockSpec(memory_space=pltpu.VMEM)
    lines = 4 * side + 2 * line
    act, in_grad, w_grad = pl.pallas_call(
        functools.partial(fused_kernel, (faces, band, size, channels), scale),
        out_shape=(
            jax.ShapeDtypeStruct((cells, channels), bf16),
            jax.ShapeDtypeStruct((cells, channels), bf16),
            jax.ShapeDtypeStruct((block, channels), f32),
        ),
        in_specs=[whole] * 5,
        out_specs=(whole,) * 3,
        scratch_shapes=[
            pltpu.VMEM((rows, channels), bf16),
            pltpu.VMEM((4, side + 2 * line, channels), bf16),
            pltpu.VMEM((4, side + 2 * line, channels), bf16),
            pltpu.VMEM((3, faces * (band + 2) * size, lines), bf16),
            pltpu.VMEM((3, faces, band + 2, size, channels), bf16),
            pltpu.VMEM((3, faces, band + 2, size, channels), bf16),
            pltpu.VMEM((rows, channels), f32),
            pltpu.VMEM((rows, channels), bf16),
            pltpu.VMEM((2, 4 * block, channels), bf16),
            pltpu.VMEM((4 * block, channels), bf16),
            pltpu.VMEM((4 * block, channels), bf16),
            pltpu.VMEM((3, block, channels), bf16),
            pltpu.VMEM((3, block, channels), bf16),
            pltpu.SemaphoreType.DMA((COPIES,)),
            pltpu.SemaphoreType.DMA((COPIES,)),
        ],
        compiler_params=pltpu.CompilerParams(
            collective_id=0, has_side_effects=True, vmem_limit_bytes=40 * 1024 * 1024
        ),
    )(
        fields.reshape(cells, channels),
        weight,
        cotangent.reshape(cells, channels),
        pad_index,
        cell_index,
    )
    return act.reshape(fields.shape), in_grad.reshape(fields.shape), w_grad


def solution(mesh):
    in_specs = (
        P(("groups", "member"), None, "tile", None, None),
        P(("tile", "member"), None),
        P(("groups", "member"), None, "tile", None, None),
        P(),
    )
    out_specs = (
        P(("groups", "member"), None, "tile", None, None),
        P(("groups", "member"), None, "tile", None, None),
        P(("groups", "tile", "member"), None),
    )
    return jax.shard_map(shards, mesh=mesh, in_specs=in_specs, out_specs=out_specs, check_vma=False)
```

```python
import functools
import math

import jax
import jax.numpy as jnp
from jax import lax
from jax.experimental import pallas as pl
from jax.experimental.pallas import tpu as pltpu
from jax.sharding import PartitionSpec as P

gelu_scale = 0.7978845608028654


def from_root(value, axis, source):
    kept = jnp.where(lax.axis_index(axis) == source, value, 0).astype(value.dtype)
    return lax.psum(kept, axis)


def extended(cells, sides, width):
    for axis, dim in sides:
        count = lax.axis_size(axis)
        ends = count - 1
        head = lax.slice_in_dim(cells, 0, width, axis=dim)
        tail = lax.slice_in_dim(cells, cells.shape[dim] - width, cells.shape[dim], axis=dim)
        cells = jnp.concatenate(
            [
                lax.ppermute(tail, axis, [(i, (i + 1) % count) for i in range(ends)]),
                cells,
                lax.ppermute(head, axis, [((i + 1) % count, i) for i in range(ends)]),
            ],
            axis=dim,
        )
    return cells


def gelu_tanh(argument):
    return (
        0.5
        * argument
        * (1.0 + jnp.tanh(gelu_scale * (argument + 0.044715 * argument * argument * argument)))
    )


def edge_selector(adjacency):
    source_index = adjacency[:, :, 2] * 24 + adjacency[:, :, 0] * 4 + adjacency[:, :, 1]
    source_index = source_index.reshape(24)
    return (source_index[:, None] == jnp.arange(48, dtype=jnp.int32)[None, :]).astype(jnp.float32)


def route_lines(cycle_grad, selector):
    members, face_count, edges, face_size, channels = cycle_grad.shape
    flat_cycle = cycle_grad.reshape(members, 24, face_size, channels)
    routed = jnp.einsum("ts,mtfc->msfc", selector, flat_cycle, precision=lax.Precision.HIGHEST)
    line_grad = routed[:, :24] + routed[:, 24:, ::-1]
    return line_grad.reshape(members, face_count, 4, face_size, channels)


def plain_shards(fields, weight, cotangent, adjacency):
    members, face_count, band_rows, face_size, channels = fields.shape
    position = lax.axis_index("tile")
    tile_count = lax.axis_size("tile")
    top_device = position == 0
    bottom_device = position == tile_count - 1
    row_start = position * band_rows
    selector = edge_selector(adjacency)
    full_weight = lax.all_gather(weight, ("tile", "member"), axis=0, tiled=True)
    side_columns = jnp.stack([fields[:, :, :, 0, :], fields[:, :, :, -1, :]], axis=2)
    all_columns = lax.all_gather(side_columns, "tile", axis=3, tiled=True)
    north_lines = from_root(fields[:, :, 0, :, :], "tile", 0)
    south_lines = from_root(fields[:, :, -1, :, :], "tile", tile_count - 1)
    edge_lines = jnp.concatenate(
        [north_lines[:, :, None], south_lines[:, :, None], all_columns], axis=2
    )
    edge_lines = edge_lines.reshape(members, 24, face_size, channels)
    both_ways = jnp.concatenate([edge_lines, edge_lines[:, :, ::-1]], axis=1)
    cycle_cells = jnp.einsum(
        "ts,msfc->mtfc",
        selector.astype(jnp.bfloat16),
        both_ways,
        preferred_element_type=jnp.float32,
    )
    cycle_cells = cycle_cells.astype(jnp.bfloat16).reshape(
        members, face_count, 4, face_size, channels
    )
    side_cycle = lax.dynamic_slice_in_dim(cycle_cells[:, :, 2:4], row_start, band_rows, 3)
    widened = jnp.concatenate(
        [side_cycle[:, :, 0][:, :, :, None], fields, side_cycle[:, :, 1][:, :, :, None]], axis=3
    )
    padded = extended(widened, (("tile", 2),), 1)
    zero_cell = jnp.zeros((members, face_count, 1, channels), jnp.bfloat16)
    north_row = jnp.concatenate([zero_cell, cycle_cells[:, :, 0], zero_cell], axis=2)
    south_row = jnp.concatenate([zero_cell, cycle_cells[:, :, 1], zero_cell], axis=2)
    padded = padded.at[:, :, 0].set(jnp.where(top_device, north_row, padded[:, :, 0]))
    padded = padded.at[:, :, -1].set(jnp.where(bottom_device, south_row, padded[:, :, -1]))
    cell_count = members * face_count * band_rows * face_size
    pre_act = jnp.zeros((cell_count, channels), jnp.float32)
    for row_step in range(3):
        for col_step in range(3):
            offset = 3 * row_step + col_step
            window = padded[
                :, :, row_step : row_step + band_rows, col_step : col_step + face_size
            ].reshape(cell_count, channels)
            pre_act = pre_act + jnp.dot(
                window,
                full_weight[offset * channels : (offset + 1) * channels],
                preferred_element_type=jnp.float32,
            )
    activation = gelu_tanh(pre_act).astype(jnp.bfloat16).reshape(fields.shape)
    unused_value, pullback = jax.vjp(gelu_tanh, pre_act)
    act_grad = pullback(cotangent.reshape(cell_count, channels).astype(jnp.float32))[0].astype(
        jnp.bfloat16
    )
    grad_terms = []
    grad_pad = jnp.zeros((members, face_count, band_rows + 2, face_size + 2, channels), jnp.float32)
    for row_step in range(3):
        for col_step in range(3):
            offset = 3 * row_step + col_step
            window = padded[
                :, :, row_step : row_step + band_rows, col_step : col_step + face_size
            ].reshape(cell_count, channels)
            grad_terms.append(
                lax.dot_general(
                    window, act_grad, (((0,), (0,)), ((), ())), preferred_element_type=jnp.float32
                )
            )
            kernel_rows = full_weight[offset * channels : (offset + 1) * channels]
            product_term = jnp.dot(act_grad, kernel_rows.T, preferred_element_type=jnp.float32)
            product_term = product_term.reshape(members, face_count, band_rows, face_size, channels)
            grad_pad = grad_pad.at[
                :, :, row_step : row_step + band_rows, col_step : col_step + face_size
            ].add(product_term)
    local_grad = jnp.concatenate(grad_terms, axis=0)
    owned_rows = lax.psum_scatter(local_grad, ("tile", "member"), scatter_dimension=0, tiled=True)
    total_cells = cell_count * tile_count * lax.axis_size("member")
    weight_grad = owned_rows / math.sqrt(total_cells)
    cycle_rows = jnp.stack([grad_pad[:, :, 0], grad_pad[:, :, -1]], axis=2)
    received = extended(cycle_rows, (("tile", 2),), 1)
    band_grad = grad_pad[:, :, 1:-1]
    band_grad = band_grad.at[:, :, 0].add(received[:, :, 0])
    band_grad = band_grad.at[:, :, -1].add(received[:, :, 3])
    side_grad = jnp.stack([band_grad[:, :, :, 0], band_grad[:, :, :, -1]], axis=2)
    side_full = lax.dynamic_update_slice_in_dim(
        jnp.zeros((members, face_count, 2, face_size, channels), jnp.float32),
        side_grad,
        row_start,
        3,
    )
    north_grad = jnp.where(top_device, grad_pad[:, :, 0, 1:-1], 0.0)
    south_grad = jnp.where(bottom_device, grad_pad[:, :, -1, 1:-1], 0.0)
    cycle_grad = jnp.concatenate(
        [north_grad[:, :, None], south_grad[:, :, None], side_full], axis=2
    )
    line_grad = route_lines(cycle_grad, selector)
    side_share = lax.psum_scatter(
        line_grad[:, :, 2:4].astype(jnp.bfloat16), "tile", scatter_dimension=3, tiled=True
    ).astype(jnp.float32)
    top_bottom = lax.psum(line_grad[:, :, 0:2].astype(jnp.bfloat16), "tile").astype(jnp.float32)
    cell_grad = band_grad[:, :, :, 1:-1]
    cell_grad = cell_grad.at[:, :, :, 0].add(side_share[:, :, 0])
    cell_grad = cell_grad.at[:, :, :, -1].add(side_share[:, :, 1])
    cell_grad = cell_grad.at[:, :, 0].add(jnp.where(top_device, top_bottom[:, :, 0], 0.0))
    cell_grad = cell_grad.at[:, :, -1].add(jnp.where(bottom_device, top_bottom[:, :, 1], 0.0))
    input_grad = cell_grad.astype(jnp.bfloat16)
    return (activation, input_grad, weight_grad)


MESH = pl.DeviceIdType.MESH
COPIES = 45
WZ, WX, WS, WD, EX, GX, R1, X2, Z3 = 0, 3, 7, 11, 15, 24, 33, 38, 42


def lane_numbers(width):
    return lax.broadcasted_iota(jnp.int32, (1, width), 1)


def placing(row_of_lane, rows):
    width = row_of_lane.shape[1]
    numbers = lax.broadcasted_iota(jnp.int32, (rows, width), 0)
    return jnp.where(numbers == row_of_lane, 1.0, 0.0).astype(jnp.bfloat16)


def store_kernel(act_ref, in_grad_ref, w_grad_ref, act_out, in_grad_out, w_grad_out, sems):
    pairs = ((act_ref, act_out), (in_grad_ref, in_grad_out), (w_grad_ref, w_grad_out))
    copies = [pltpu.make_async_copy(a, b, sems.at[i]) for i, (a, b) in enumerate(pairs)]
    for copy in copies:
        copy.start()
    for copy in copies:
        copy.wait()


def fused_kernel(
    dims,
    scale,
    fields_ref,
    weight_ref,
    cot_ref,
    adjacency_ref,
    act_ref,
    in_grad_ref,
    w_grad_ref,
    full_w,
    edges,
    grad_edges,
    cross,
    padded,
    shifted,
    total,
    outgoing,
    from_core,
    to_x,
    from_x,
    to_z,
    from_z,
    send_sem,
    recv_sem,
):
    faces, band, size, channels = dims
    cells = faces * band * size
    line = faces * size
    side = faces * 2 * band
    block = weight_ref.shape[0]
    quarter = 4 * block
    f32, bf16 = jnp.float32, jnp.bfloat16
    me = lax.axis_index("tile")
    z = lax.axis_index("member")
    chip, core = me // 2, me % 2
    sib = chip * 2 + (1 - core)
    across = (1 - chip) * 2 + core
    diag = (1 - chip) * 2 + (1 - core)
    tile_peers = (sib, across, diag)

    def remote(src, dst, sem, target):
        return pltpu.make_async_remote_copy(
            src_ref=src,
            dst_ref=dst,
            send_sem=send_sem.at[sem],
            recv_sem=recv_sem.at[sem],
            device_id=target,
            device_id_type=MESH,
        )

    def tile_id(t):
        return {"tile": t}

    def member_id(k):
        return {"member": (z + k) % 4}

    def w_block(t, m):
        return full_w.at[pl.ds(pl.multiple_of((t * 4 + m) * block, 16), block)]

    def edge_parts(buf, first, source, target):
        top = (source == 0) | (target == source - 1)
        bottom = (source == 3) | (target == source + 1)
        spans = ((0, side, None), (side, line, top), (side + line, line, bottom))
        for part, (start, count, needed) in enumerate(spans):
            piece = buf.at[source, pl.ds(start, count)]
            yield needed, piece, first + part

    def when(needed, action):
        if needed is None:
            action()
        else:
            pl.when(needed)(action)

    def each_edge(buf, first, incoming, action):
        for k, t in enumerate(tile_peers):
            source, target = (t, me) if incoming else (me, t)
            for needed, piece, sem in edge_parts(buf, first + 3 * k, source, target):
                when(needed, functools.partial(action, remote(piece, piece, sem, tile_id(t))))

    def send_edges(buf, first):
        each_edge(buf, first, False, lambda copy: copy.start())

    def take_edges(buf, first):
        each_edge(buf, first, True, lambda copy: copy.wait_recv())

    def finish_edges(buf, first):
        each_edge(buf, first, False, lambda copy: copy.wait_send())

    barrier = pltpu.get_barrier_semaphore()
    for t in tile_peers:
        pl.semaphore_signal(barrier, inc=1, device_id=tile_id(t), device_id_type=MESH)
    for k in range(1, 4):
        pl.semaphore_signal(barrier, inc=1, device_id=member_id(k), device_id_type=MESH)

    row_start = me * band
    q = lane_numbers(cells)
    col, row, face = q % size, (q // size) % band, q // (size * band)
    target = face * (2 * band) + row + jnp.where(col == 0, 0, band)
    side_pick = placing(jnp.where((col == 0) | (col == size - 1), target, -1), side)

    def own_edges(values, out):
        cube = values.reshape(faces, band, size, channels)
        out[me, 0:side] = jnp.dot(side_pick, values, preferred_element_type=f32).astype(bf16)
        out[me, side : side + line] = cube[:, 0].reshape(line, channels)
        out[me, side + line : side + 2 * line] = cube[:, band - 1].reshape(line, channels)

    w_block(me, z)[...] = weight_ref[...]
    own_edges(fields_ref[...], edges)
    pl.semaphore_wait(barrier, 6)

    started = []

    def go(copy):
        copy.start()
        started.append(copy)

    for k in (2, 1, 3):
        go(remote(w_block(me, z), w_block(me, z), WZ + k - 1, member_id(k)))
    send_edges(edges, EX)

    def w_spread(k):
        part = w_block(me, (z + 4 - k) % 4)
        if k:
            remote(part, part, WZ + k - 1, member_id(k)).wait_recv()
        go(remote(part, part, WX + k, tile_id(across)))
        go(remote(part, part, WS + k, tile_id(sib)))

    w_spread(0)
    q = lane_numbers(4 * line)
    bank, along = q // size, q % size
    base, turned = jnp.zeros_like(q), jnp.zeros_like(q)
    for f in range(faces):
        for e in range(4):
            first = 3 * (4 * f + e)
            here = bank == e * faces + f
            start = adjacency_ref[first + 1] * line + adjacency_ref[first] * size
            base = jnp.where(here, start, base)
            turned = jnp.where(here, adjacency_ref[first + 2], turned)
    cross[...] = placing(base + along + turned * (size - 1 - 2 * along), 4 * line)
    q = lane_numbers(4 * side)
    band_of, rest = q // side, q % side
    order = placing(
        ((rest // band) % 2) * line
        + (rest // (2 * band)) * size
        + band_of * band
        + rest % band,
        2 * line,
    )
    for k in (1, 3, 2):
        w_spread(k)

    def columns(rows):
        return lax.broadcasted_iota(jnp.int32, (rows, 1), 0) % size

    def moved(values, step):
        rows = values.shape[0]
        if step == 0:
            return values
        if step < 0:
            return jnp.where(columns(rows) == 0, 0.0, pltpu.roll(values, 1, 0))
        return jnp.where(columns(rows) == size - 1, 0.0, pltpu.roll(values, rows - 1, 0))

    def with_halo(values, buf, north, south):
        above = buf[jnp.maximum(me - 1, 0), side + line : side + 2 * line].astype(f32)
        below = buf[jnp.minimum(me + 1, 3), side : side + line].astype(f32)
        above = jnp.where(me > 0, above, north).reshape(faces, 1, size, channels)
        below = jnp.where(me < 3, below, south).reshape(faces, 1, size, channels)
        own = values.astype(f32).reshape(faces, band, size, channels)
        return jnp.concatenate([above, own, below], axis=1).reshape(-1, channels)

    def lines_of(buf):
        sides = jnp.concatenate([buf[t, 0:side] for t in range(4)], axis=0)
        sides = jnp.dot(order, sides, preferred_element_type=f32).astype(bf16)
        north = buf[0, side : side + line]
        south = buf[3, side + line : side + 2 * line]
        return jnp.concatenate([north, south, sides], axis=0)

    take_edges(edges, EX)
    cycle_cells = jnp.dot(cross[...], lines_of(edges), preferred_element_type=f32)
    center = with_halo(
        fields_ref[...], edges, cycle_cells[0:line], cycle_cells[line : 2 * line]
    )
    cycle_sides = cycle_cells[2 * line :].astype(bf16)
    q = lane_numbers(line)
    near = q % size - row_start + 1
    spot = (q // size) * ((band + 2) * size) + near * size
    inside = (near >= 0) & (near < band + 2)
    for dx in range(3):
        values = moved(center, dx - 1)
        if dx != 1:
            first = line if dx else 0
            put = placing(
                jnp.where(inside, spot + (size - 1 if dx else 0), -1), faces * (band + 2) * size
            )
            values = values + jnp.dot(
                put, cycle_sides[first : first + line], preferred_element_type=f32
            )
        padded[dx] = values.astype(bf16).reshape(faces, band + 2, size, channels)

    for k in (0, 1, 3, 2):
        part = w_block(across, (z + 4 - k) % 4)
        remote(part, part, WX + k, tile_id(across)).wait_recv()
        go(remote(part, part, WD + k, tile_id(sib)))
    for k in range(4):
        part = w_block(sib, (z + 4 - k) % 4)
        remote(part, part, WS + k, tile_id(sib)).wait_recv()
        part = w_block(diag, (z + 4 - k) % 4)
        remote(part, part, WD + k, tile_id(sib)).wait_recv()

    def window(dy, dx):
        return padded[dx, :, dy : dy + band].reshape(cells, channels)

    def w_of(dy, dx):
        first = (3 * dy + dx) * channels
        return full_w[first : first + channels]

    pre = jnp.zeros((cells, channels), f32)
    for dy in range(3):
        for dx in range(3):
            pre = pre + jnp.dot(window(dy, dx), w_of(dy, dx), preferred_element_type=f32)
    square = pre * pre
    bend = jnp.tanh(gelu_scale * (pre + 0.044715 * pre * square))
    act_ref[...] = (0.5 * pre * (1.0 + bend)).astype(bf16)
    slope = 0.5 * (1.0 + bend) + 0.5 * pre * (1.0 - bend * bend) * (
        gelu_scale * (1.0 + 3 * 0.044715 * square)
    )
    act_grad = (cot_ref[...].astype(f32) * slope).astype(bf16)
    own_edges(act_grad, grad_edges)
    send_edges(grad_edges, GX)

    for dy in range(3):
        for dx in range(3):
            first = (3 * dy + dx) * channels
            part = lax.dot_general(
                window(dy, dx), act_grad, (((0,), (0,)), ((), ())), preferred_element_type=f32
            )
            total[first : first + channels] = part
            outgoing[first : first + channels] = part.astype(bf16)

    def quarter_at(t):
        return pl.ds(pl.multiple_of(t * quarter, 16), quarter)

    def part_at(m):
        return pl.ds(pl.multiple_of(m * block, 16), block)

    def row_at(t, m):
        return pl.ds(pl.multiple_of((t * 4 + m) * block, 16), block)

    for k in (2, 1, 3, 0):
        m = (z + k) % 4
        there = from_core.at[0, part_at(m)]
        go(remote(outgoing.at[row_at(diag, m)], there, R1 + k, tile_id(sib)))
    go(remote(outgoing.at[quarter_at(sib)], from_core.at[1], R1 + 4, tile_id(sib)))

    for k in (2, 1, 3, 0):
        m = (z + k) % 4
        there = from_core.at[0, part_at(m)]
        remote(there, there, R1 + k, tile_id(sib)).wait_recv()
        to_x[part_at(m)] = (
            total[row_at(across, m)] + from_core[0, part_at(m)].astype(f32)
        ).astype(bf16)
        go(remote(to_x.at[part_at(m)], from_x.at[part_at(m)], X2 + k, tile_id(across)))

    take_edges(grad_edges, GX)
    center = with_halo(act_grad, grad_edges, 0.0, 0.0)
    for dx in range(3):
        shifted[dx] = (
            moved(center, 1 - dx).astype(bf16).reshape(faces, band + 2, size, channels)
        )
    grad = jnp.zeros((cells, channels), f32)
    over_outputs = (((1,), (1,)), ((), ()))
    for dy in range(3):
        for dx in range(3):
            grad = grad + lax.dot_general(
                shifted[dx, :, 2 - dy : 2 - dy + band].reshape(cells, channels),
                w_of(dy, dx),
                over_outputs,
                preferred_element_type=f32,
            )

    remote(from_core.at[1], from_core.at[1], R1 + 4, tile_id(sib)).wait_recv()
    for k in (2, 1, 3, 0):
        m = (z + k) % 4
        remote(to_x.at[part_at(m)], from_x.at[part_at(m)], X2 + k, tile_id(across)).wait_recv()
        mine = (
            total[row_at(me, m)]
            + from_core[1, part_at(m)].astype(f32)
            + from_x[part_at(m)].astype(f32)
        )
        if k:
            to_z[k - 1] = mine.astype(bf16)
            go(remote(to_z.at[k - 1], from_z.at[k - 1], Z3 + k - 1, member_id(k)))
        else:
            w_grad_ref[...] = mine

    lines = lines_of(grad_edges).astype(f32)
    taps = [moved(lines, 1 - s).astype(bf16) for s in range(3)]
    pieces = []
    for edge in range(4):
        piece = jnp.zeros((line, channels), f32)
        for s in range(3):
            dy, dx = ((0, s), (2, s), (s, 0), (s, 2))[edge]
            piece = piece + lax.dot_general(
                taps[s][edge * line : (edge + 1) * line],
                w_of(dy, dx),
                over_outputs,
                preferred_element_type=f32,
            )
        pieces.append(piece)
    cycle = jnp.concatenate(pieces, axis=0)
    high = cycle.astype(bf16)
    low = (cycle - high.astype(f32)).astype(bf16)
    q = lane_numbers(2 * line)
    lane_face, near = (q // size) % faces, q % size - row_start
    spot = lane_face * (band * size) + near * size + jnp.where(q < line, 0, size - 1)
    put = placing(jnp.where((near >= 0) & (near < band), spot, -1), cells)
    grad = grad.reshape(faces, band, size, channels)
    line_grad = jnp.zeros((4 * line, channels), f32)
    side_grad = jnp.zeros((cells, channels), f32)
    for level in (high, low):
        routed = jnp.dot(cross[...], level, preferred_element_type=f32)
        line_grad = line_grad + routed
        side_grad = side_grad + jnp.dot(
            put, routed[2 * line :].astype(bf16), preferred_element_type=f32
        )
    north = jnp.where(me == 0, line_grad[0:line], 0.0).reshape(faces, 1, size, channels)
    south = jnp.where(me == 3, line_grad[line : 2 * line], 0.0).reshape(faces, 1, size, channels)
    inner = jnp.zeros((faces, band - 2, size, channels), f32)
    grad = grad + jnp.concatenate([north, inner, south], axis=1)
    grad = grad.reshape(cells, channels) + side_grad
    in_grad_ref[...] = grad.astype(bf16)

    result = w_grad_ref[...]
    for k in range(1, 4):
        remote(from_z.at[k - 1], from_z.at[k - 1], Z3 + k - 1, member_id(k)).wait_recv()
        result = result + from_z[k - 1].astype(f32)
    w_grad_ref[...] = result * scale
    finish_edges(edges, EX)
    finish_edges(grad_edges, GX)
    for copy in started:
        copy.wait_send()


def shards(fields, weight, cotangent, adjacency):
    members, faces, band, size, channels = fields.shape
    tiles, across = lax.axis_size("tile"), lax.axis_size("member")
    block = weight.shape[0]
    fits = tiles == 4 and across == 4 and members == 1 and band * tiles == size
    if not (fits and size == 16 and block % 16 == 0 and (faces * 2 * band) % 16 == 0):
        return plain_shards(fields, weight, cotangent, adjacency)
    cells = faces * band * size
    side, line = faces * 2 * band, faces * size
    bf16, f32 = jnp.bfloat16, jnp.float32
    scale = 1.0 / math.sqrt(cells * tiles * across)
    rows = block * tiles * across
    whole = pl.BlockSpec(memory_space=pltpu.VMEM)
    results = pl.pallas_call(
        functools.partial(fused_kernel, (faces, band, size, channels), scale),
        out_shape=(
            jax.ShapeDtypeStruct((cells, channels), bf16),
            jax.ShapeDtypeStruct((cells, channels), bf16),
            jax.ShapeDtypeStruct((block, channels), f32),
        ),
        in_specs=[whole] * 3 + [pl.BlockSpec(memory_space=pltpu.SMEM)],
        out_specs=(whole,) * 3,
        scratch_shapes=[
            pltpu.VMEM((rows, channels), bf16),
            pltpu.VMEM((4, side + 2 * line, channels), bf16),
            pltpu.VMEM((4, side + 2 * line, channels), bf16),
            pltpu.VMEM((4 * line, 4 * line), bf16),
            pltpu.VMEM((3, faces, band + 2, size, channels), bf16),
            pltpu.VMEM((3, faces, band + 2, size, channels), bf16),
            pltpu.VMEM((rows, channels), f32),
            pltpu.VMEM((rows, channels), bf16),
            pltpu.VMEM((2, 4 * block, channels), bf16),
            pltpu.VMEM((4 * block, channels), bf16),
            pltpu.VMEM((4 * block, channels), bf16),
            pltpu.VMEM((3, block, channels), bf16),
            pltpu.VMEM((3, block, channels), bf16),
            pltpu.SemaphoreType.DMA((COPIES,)),
            pltpu.SemaphoreType.DMA((COPIES,)),
        ],
        compiler_params=pltpu.CompilerParams(
            collective_id=0, has_side_effects=True, vmem_limit_bytes=40 * 1024 * 1024
        ),
    )(
        fields.reshape(cells, channels),
        weight,
        cotangent.reshape(cells, channels),
        adjacency.reshape(-1),
    )
    anywhere = pl.BlockSpec(memory_space=pl.ANY)
    act, in_grad, w_grad = pl.pallas_call(
        store_kernel,
        out_shape=tuple(jax.ShapeDtypeStruct(r.shape, r.dtype) for r in results),
        in_specs=[whole] * 3,
        out_specs=(anywhere,) * 3,
        scratch_shapes=[pltpu.SemaphoreType.DMA((3,))],
    )(*results)
    return act.reshape(fields.shape), in_grad.reshape(fields.shape), w_grad


def solution(mesh):
    in_specs = (
        P(("groups", "member"), None, "tile", None, None),
        P(("tile", "member"), None),
        P(("groups", "member"), None, "tile", None, None),
        P(),
    )
    out_specs = (
        P(("groups", "member"), None, "tile", None, None),
        P(("groups", "member"), None, "tile", None, None),
        P(("groups", "tile", "member"), None),
    )
    return jax.shard_map(shards, mesh=mesh, in_specs=in_specs, out_specs=out_specs, check_vma=False)
```

```python
import functools
import math

import jax
import jax.numpy as jnp
from jax import lax
from jax.experimental import pallas as pl
from jax.experimental.pallas import tpu as pltpu
from jax.sharding import PartitionSpec as P

gelu_scale = 0.7978845608028654


def from_root(value, axis, source):
    kept = jnp.where(lax.axis_index(axis) == source, value, 0).astype(value.dtype)
    return lax.psum(kept, axis)


def extended(cells, sides, width):
    for axis, dim in sides:
        count = lax.axis_size(axis)
        ends = count - 1
        head = lax.slice_in_dim(cells, 0, width, axis=dim)
        tail = lax.slice_in_dim(cells, cells.shape[dim] - width, cells.shape[dim], axis=dim)
        cells = jnp.concatenate(
            [
                lax.ppermute(tail, axis, [(i, (i + 1) % count) for i in range(ends)]),
                cells,
                lax.ppermute(head, axis, [((i + 1) % count, i) for i in range(ends)]),
            ],
            axis=dim,
        )
    return cells


def gelu_tanh(argument):
    return (
        0.5
        * argument
        * (1.0 + jnp.tanh(gelu_scale * (argument + 0.044715 * argument * argument * argument)))
    )


def edge_selector(adjacency):
    source_index = adjacency[:, :, 2] * 24 + adjacency[:, :, 0] * 4 + adjacency[:, :, 1]
    source_index = source_index.reshape(24)
    return (source_index[:, None] == jnp.arange(48, dtype=jnp.int32)[None, :]).astype(jnp.float32)


def route_lines(cycle_grad, selector):
    members, face_count, edges, face_size, channels = cycle_grad.shape
    flat_cycle = cycle_grad.reshape(members, 24, face_size, channels)
    routed = jnp.einsum("ts,mtfc->msfc", selector, flat_cycle, precision=lax.Precision.HIGHEST)
    line_grad = routed[:, :24] + routed[:, 24:, ::-1]
    return line_grad.reshape(members, face_count, 4, face_size, channels)


def plain_shards(fields, weight, cotangent, adjacency):
    members, face_count, band_rows, face_size, channels = fields.shape
    position = lax.axis_index("tile")
    tile_count = lax.axis_size("tile")
    top_device = position == 0
    bottom_device = position == tile_count - 1
    row_start = position * band_rows
    selector = edge_selector(adjacency)
    full_weight = lax.all_gather(weight, ("tile", "member"), axis=0, tiled=True)
    side_columns = jnp.stack([fields[:, :, :, 0, :], fields[:, :, :, -1, :]], axis=2)
    all_columns = lax.all_gather(side_columns, "tile", axis=3, tiled=True)
    north_lines = from_root(fields[:, :, 0, :, :], "tile", 0)
    south_lines = from_root(fields[:, :, -1, :, :], "tile", tile_count - 1)
    edge_lines = jnp.concatenate(
        [north_lines[:, :, None], south_lines[:, :, None], all_columns], axis=2
    )
    edge_lines = edge_lines.reshape(members, 24, face_size, channels)
    both_ways = jnp.concatenate([edge_lines, edge_lines[:, :, ::-1]], axis=1)
    cycle_cells = jnp.einsum(
        "ts,msfc->mtfc",
        selector.astype(jnp.bfloat16),
        both_ways,
        preferred_element_type=jnp.float32,
    )
    cycle_cells = cycle_cells.astype(jnp.bfloat16).reshape(
        members, face_count, 4, face_size, channels
    )
    side_cycle = lax.dynamic_slice_in_dim(cycle_cells[:, :, 2:4], row_start, band_rows, 3)
    widened = jnp.concatenate(
        [side_cycle[:, :, 0][:, :, :, None], fields, side_cycle[:, :, 1][:, :, :, None]], axis=3
    )
    padded = extended(widened, (("tile", 2),), 1)
    zero_cell = jnp.zeros((members, face_count, 1, channels), jnp.bfloat16)
    north_row = jnp.concatenate([zero_cell, cycle_cells[:, :, 0], zero_cell], axis=2)
    south_row = jnp.concatenate([zero_cell, cycle_cells[:, :, 1], zero_cell], axis=2)
    padded = padded.at[:, :, 0].set(jnp.where(top_device, north_row, padded[:, :, 0]))
    padded = padded.at[:, :, -1].set(jnp.where(bottom_device, south_row, padded[:, :, -1]))
    cell_count = members * face_count * band_rows * face_size
    pre_act = jnp.zeros((cell_count, channels), jnp.float32)
    for row_step in range(3):
        for col_step in range(3):
            offset = 3 * row_step + col_step
            window = padded[
                :, :, row_step : row_step + band_rows, col_step : col_step + face_size
            ].reshape(cell_count, channels)
            pre_act = pre_act + jnp.dot(
                window,
                full_weight[offset * channels : (offset + 1) * channels],
                preferred_element_type=jnp.float32,
            )
    activation = gelu_tanh(pre_act).astype(jnp.bfloat16).reshape(fields.shape)
    unused_value, pullback = jax.vjp(gelu_tanh, pre_act)
    act_grad = pullback(cotangent.reshape(cell_count, channels).astype(jnp.float32))[0].astype(
        jnp.bfloat16
    )
    grad_terms = []
    grad_pad = jnp.zeros((members, face_count, band_rows + 2, face_size + 2, channels), jnp.float32)
    for row_step in range(3):
        for col_step in range(3):
            offset = 3 * row_step + col_step
            window = padded[
                :, :, row_step : row_step + band_rows, col_step : col_step + face_size
            ].reshape(cell_count, channels)
            grad_terms.append(
                lax.dot_general(
                    window, act_grad, (((0,), (0,)), ((), ())), preferred_element_type=jnp.float32
                )
            )
            kernel_rows = full_weight[offset * channels : (offset + 1) * channels]
            product_term = jnp.dot(act_grad, kernel_rows.T, preferred_element_type=jnp.float32)
            product_term = product_term.reshape(members, face_count, band_rows, face_size, channels)
            grad_pad = grad_pad.at[
                :, :, row_step : row_step + band_rows, col_step : col_step + face_size
            ].add(product_term)
    local_grad = jnp.concatenate(grad_terms, axis=0)
    owned_rows = lax.psum_scatter(local_grad, ("tile", "member"), scatter_dimension=0, tiled=True)
    total_cells = cell_count * tile_count * lax.axis_size("member")
    weight_grad = owned_rows / math.sqrt(total_cells)
    cycle_rows = jnp.stack([grad_pad[:, :, 0], grad_pad[:, :, -1]], axis=2)
    received = extended(cycle_rows, (("tile", 2),), 1)
    band_grad = grad_pad[:, :, 1:-1]
    band_grad = band_grad.at[:, :, 0].add(received[:, :, 0])
    band_grad = band_grad.at[:, :, -1].add(received[:, :, 3])
    side_grad = jnp.stack([band_grad[:, :, :, 0], band_grad[:, :, :, -1]], axis=2)
    side_full = lax.dynamic_update_slice_in_dim(
        jnp.zeros((members, face_count, 2, face_size, channels), jnp.float32),
        side_grad,
        row_start,
        3,
    )
    north_grad = jnp.where(top_device, grad_pad[:, :, 0, 1:-1], 0.0)
    south_grad = jnp.where(bottom_device, grad_pad[:, :, -1, 1:-1], 0.0)
    cycle_grad = jnp.concatenate(
        [north_grad[:, :, None], south_grad[:, :, None], side_full], axis=2
    )
    line_grad = route_lines(cycle_grad, selector)
    side_share = lax.psum_scatter(
        line_grad[:, :, 2:4].astype(jnp.bfloat16), "tile", scatter_dimension=3, tiled=True
    ).astype(jnp.float32)
    top_bottom = lax.psum(line_grad[:, :, 0:2].astype(jnp.bfloat16), "tile").astype(jnp.float32)
    cell_grad = band_grad[:, :, :, 1:-1]
    cell_grad = cell_grad.at[:, :, :, 0].add(side_share[:, :, 0])
    cell_grad = cell_grad.at[:, :, :, -1].add(side_share[:, :, 1])
    cell_grad = cell_grad.at[:, :, 0].add(jnp.where(top_device, top_bottom[:, :, 0], 0.0))
    cell_grad = cell_grad.at[:, :, -1].add(jnp.where(bottom_device, top_bottom[:, :, 1], 0.0))
    input_grad = cell_grad.astype(jnp.bfloat16)
    return (activation, input_grad, weight_grad)


MESH = pl.DeviceIdType.MESH
COPIES = 45
WZ, WX, WS, WD, EX, GX, R1, X2, Z3 = 0, 3, 7, 11, 15, 24, 33, 38, 42


def lane_numbers(width):
    return lax.broadcasted_iota(jnp.int32, (1, width), 1)


def placing(row_of_lane, rows):
    width = row_of_lane.shape[1]
    numbers = lax.broadcasted_iota(jnp.int32, (rows, width), 0)
    return jnp.where(numbers == row_of_lane, 1.0, 0.0).astype(jnp.bfloat16)


def store_kernel(act_ref, in_grad_ref, w_grad_ref, act_out, in_grad_out, w_grad_out, sems):
    pairs = ((act_ref, act_out), (in_grad_ref, in_grad_out), (w_grad_ref, w_grad_out))
    copies = [pltpu.make_async_copy(a, b, sems.at[i]) for i, (a, b) in enumerate(pairs)]
    for copy in copies:
        copy.start()
    for copy in copies:
        copy.wait()


def fused_kernel(
    dims,
    scale,
    fields_hbm,
    weight_hbm,
    cot_hbm,
    adjacency_ref,
    act_hbm,
    in_grad_hbm,
    w_grad_hbm,
    act_ref,
    in_grad_ref,
    w_grad_ref,
    fields_ref,
    cot_ref,
    full_w,
    edges,
    grad_edges,
    cross,
    padded,
    shifted,
    total,
    outgoing,
    from_core,
    to_x,
    from_x,
    to_z,
    from_z,
    send_sem,
    recv_sem,
    load_sem,
):
    faces, band, size, channels = dims
    cells = faces * band * size
    line = faces * size
    side = faces * 2 * band
    block = weight_hbm.shape[0]
    quarter = 4 * block
    f32, bf16 = jnp.float32, jnp.bfloat16
    me = lax.axis_index("tile")
    z = lax.axis_index("member")
    chip, core = me // 2, me % 2
    sib = chip * 2 + (1 - core)
    across = (1 - chip) * 2 + core
    diag = (1 - chip) * 2 + (1 - core)
    tile_peers = (sib, across, diag)

    def remote(src, dst, sem, target):
        return pltpu.make_async_remote_copy(
            src_ref=src,
            dst_ref=dst,
            send_sem=send_sem.at[sem],
            recv_sem=recv_sem.at[sem],
            device_id=target,
            device_id_type=MESH,
        )

    def tile_id(t):
        return {"tile": t}

    def member_id(k):
        return {"member": (z + k) % 4}

    def w_block(t, m):
        return full_w.at[pl.ds(pl.multiple_of((t * 4 + m) * block, 16), block)]

    def edge_parts(buf, first, source, target):
        top = (source == 0) | (target == source - 1)
        bottom = (source == 3) | (target == source + 1)
        spans = ((0, side, None), (side, line, top), (side + line, line, bottom))
        for part, (start, count, needed) in enumerate(spans):
            piece = buf.at[source, pl.ds(start, count)]
            yield needed, piece, first + part

    def when(needed, action):
        if needed is None:
            action()
        else:
            pl.when(needed)(action)

    def each_edge(buf, first, incoming, action):
        for k, t in enumerate(tile_peers):
            source, target = (t, me) if incoming else (me, t)
            for needed, piece, sem in edge_parts(buf, first + 3 * k, source, target):
                when(needed, functools.partial(action, remote(piece, piece, sem, tile_id(t))))

    def send_edges(buf, first):
        each_edge(buf, first, False, lambda copy: copy.start())

    def take_edges(buf, first):
        each_edge(buf, first, True, lambda copy: copy.wait_recv())

    def finish_edges(buf, first):
        each_edge(buf, first, False, lambda copy: copy.wait_send())

    load_w = pltpu.make_async_copy(weight_hbm, w_block(me, z), load_sem.at[0])
    load_fields = pltpu.make_async_copy(fields_hbm, fields_ref, load_sem.at[1])
    load_cot = pltpu.make_async_copy(cot_hbm, cot_ref, load_sem.at[2])
    for load in (load_w, load_fields, load_cot):
        load.start()

    barrier = pltpu.get_barrier_semaphore()
    for t in tile_peers:
        pl.semaphore_signal(barrier, inc=1, device_id=tile_id(t), device_id_type=MESH)
    for k in range(1, 4):
        pl.semaphore_signal(barrier, inc=1, device_id=member_id(k), device_id_type=MESH)

    row_start = me * band
    q = lane_numbers(cells)
    col, row, face = q % size, (q // size) % band, q // (size * band)
    target = face * (2 * band) + row + jnp.where(col == 0, 0, band)
    side_pick = placing(jnp.where((col == 0) | (col == size - 1), target, -1), side)

    def own_edges(values, out):
        cube = values.reshape(faces, band, size, channels)
        out[me, 0:side] = jnp.dot(side_pick, values, preferred_element_type=f32).astype(bf16)
        out[me, side : side + line] = cube[:, 0].reshape(line, channels)
        out[me, side + line : side + 2 * line] = cube[:, band - 1].reshape(line, channels)

    load_w.wait()
    pl.semaphore_wait(barrier, 6)

    started = []

    def go(copy):
        copy.start()
        started.append(copy)

    for k in (2, 1, 3):
        go(remote(w_block(me, z), w_block(me, z), WZ + k - 1, member_id(k)))
    load_fields.wait()
    own_edges(fields_ref[...], edges)
    send_edges(edges, EX)

    def w_spread(k):
        part = w_block(me, (z + 4 - k) % 4)
        if k:
            remote(part, part, WZ + k - 1, member_id(k)).wait_recv()
        go(remote(part, part, WX + k, tile_id(across)))
        go(remote(part, part, WS + k, tile_id(sib)))

    w_spread(0)
    q = lane_numbers(4 * line)
    bank, along = q // size, q % size
    base, turned = jnp.zeros_like(q), jnp.zeros_like(q)
    for f in range(faces):
        for e in range(4):
            here = bank == e * faces + f
            start = adjacency_ref[1, e, f] * line + adjacency_ref[0, e, f] * size
            base = jnp.where(here, start, base)
            turned = jnp.where(here, adjacency_ref[2, e, f], turned)
    cross[...] = placing(base + along + turned * (size - 1 - 2 * along), 4 * line)
    q = lane_numbers(4 * side)
    band_of, rest = q // side, q % side
    order = placing(
        ((rest // band) % 2) * line
        + (rest // (2 * band)) * size
        + band_of * band
        + rest % band,
        2 * line,
    )
    for k in (1, 3, 2):
        w_spread(k)

    def columns(rows):
        return lax.broadcasted_iota(jnp.int32, (rows, 1), 0) % size

    def moved(values, step):
        rows = values.shape[0]
        if step == 0:
            return values
        if step < 0:
            return jnp.where(columns(rows) == 0, 0.0, pltpu.roll(values, 1, 0))
        return jnp.where(columns(rows) == size - 1, 0.0, pltpu.roll(values, rows - 1, 0))

    def with_halo(values, buf, north, south):
        above = buf[jnp.maximum(me - 1, 0), side + line : side + 2 * line].astype(f32)
        below = buf[jnp.minimum(me + 1, 3), side : side + line].astype(f32)
        above = jnp.where(me > 0, above, north).reshape(faces, 1, size, channels)
        below = jnp.where(me < 3, below, south).reshape(faces, 1, size, channels)
        own = values.astype(f32).reshape(faces, band, size, channels)
        return jnp.concatenate([above, own, below], axis=1).reshape(-1, channels)

    def lines_of(buf):
        sides = jnp.concatenate([buf[t, 0:side] for t in range(4)], axis=0)
        sides = jnp.dot(order, sides, preferred_element_type=f32).astype(bf16)
        north = buf[0, side : side + line]
        south = buf[3, side + line : side + 2 * line]
        return jnp.concatenate([north, south, sides], axis=0)

    take_edges(edges, EX)
    cycle_cells = jnp.dot(cross[...], lines_of(edges), preferred_element_type=f32)
    center = with_halo(
        fields_ref[...], edges, cycle_cells[0:line], cycle_cells[line : 2 * line]
    )
    cycle_sides = cycle_cells[2 * line :].astype(bf16)
    q = lane_numbers(line)
    near = q % size - row_start + 1
    spot = (q // size) * ((band + 2) * size) + near * size
    inside = (near >= 0) & (near < band + 2)
    for dx in range(3):
        values = moved(center, dx - 1)
        if dx != 1:
            first = line if dx else 0
            put = placing(
                jnp.where(inside, spot + (size - 1 if dx else 0), -1), faces * (band + 2) * size
            )
            values = values + jnp.dot(
                put, cycle_sides[first : first + line], preferred_element_type=f32
            )
        padded[dx] = values.astype(bf16).reshape(faces, band + 2, size, channels)

    for k in (0, 1, 3, 2):
        part = w_block(across, (z + 4 - k) % 4)
        remote(part, part, WX + k, tile_id(across)).wait_recv()
        go(remote(part, part, WD + k, tile_id(sib)))
    for k in range(4):
        part = w_block(sib, (z + 4 - k) % 4)
        remote(part, part, WS + k, tile_id(sib)).wait_recv()
        part = w_block(diag, (z + 4 - k) % 4)
        remote(part, part, WD + k, tile_id(sib)).wait_recv()

    def window(dy, dx):
        return padded[dx, :, dy : dy + band].reshape(cells, channels)

    def w_of(dy, dx):
        first = (3 * dy + dx) * channels
        return full_w[first : first + channels]

    pre = jnp.zeros((cells, channels), f32)
    for dy in range(3):
        for dx in range(3):
            pre = pre + jnp.dot(window(dy, dx), w_of(dy, dx), preferred_element_type=f32)
    load_cot.wait()
    square = pre * pre
    bend = jnp.tanh(gelu_scale * (pre + 0.044715 * pre * square))
    act_ref[...] = (0.5 * pre * (1.0 + bend)).astype(bf16)
    keep_act = pltpu.make_async_copy(act_ref, act_hbm, load_sem.at[3])
    keep_act.start()
    slope = 0.5 * (1.0 + bend) + 0.5 * pre * (1.0 - bend * bend) * (
        gelu_scale * (1.0 + 3 * 0.044715 * square)
    )
    act_grad = (cot_ref[...].astype(f32) * slope).astype(bf16)
    own_edges(act_grad, grad_edges)
    send_edges(grad_edges, GX)

    for dy in range(3):
        for dx in range(3):
            first = (3 * dy + dx) * channels
            part = lax.dot_general(
                window(dy, dx), act_grad, (((0,), (0,)), ((), ())), preferred_element_type=f32
            )
            total[first : first + channels] = part
            outgoing[first : first + channels] = part.astype(bf16)

    def quarter_at(t):
        return pl.ds(pl.multiple_of(t * quarter, 16), quarter)

    def part_at(m):
        return pl.ds(pl.multiple_of(m * block, 16), block)

    def row_at(t, m):
        return pl.ds(pl.multiple_of((t * 4 + m) * block, 16), block)

    for k in (2, 1, 3, 0):
        m = (z + k) % 4
        there = from_core.at[0, part_at(m)]
        go(remote(outgoing.at[row_at(diag, m)], there, R1 + k, tile_id(sib)))
    go(remote(outgoing.at[quarter_at(sib)], from_core.at[1], R1 + 4, tile_id(sib)))

    for k in (2, 1, 3, 0):
        m = (z + k) % 4
        there = from_core.at[0, part_at(m)]
        remote(there, there, R1 + k, tile_id(sib)).wait_recv()
        to_x[part_at(m)] = (
            total[row_at(across, m)] + from_core[0, part_at(m)].astype(f32)
        ).astype(bf16)
        go(remote(to_x.at[part_at(m)], from_x.at[part_at(m)], X2 + k, tile_id(across)))

    take_edges(grad_edges, GX)
    center = with_halo(act_grad, grad_edges, 0.0, 0.0)
    for dx in range(3):
        shifted[dx] = (
            moved(center, 1 - dx).astype(bf16).reshape(faces, band + 2, size, channels)
        )
    grad = jnp.zeros((cells, channels), f32)
    over_outputs = (((1,), (1,)), ((), ()))
    for dy in range(3):
        for dx in range(3):
            grad = grad + lax.dot_general(
                shifted[dx, :, 2 - dy : 2 - dy + band].reshape(cells, channels),
                w_of(dy, dx),
                over_outputs,
                preferred_element_type=f32,
            )

    remote(from_core.at[1], from_core.at[1], R1 + 4, tile_id(sib)).wait_recv()
    for k in (2, 1, 3, 0):
        m = (z + k) % 4
        remote(to_x.at[part_at(m)], from_x.at[part_at(m)], X2 + k, tile_id(across)).wait_recv()
        mine = (
            total[row_at(me, m)]
            + from_core[1, part_at(m)].astype(f32)
            + from_x[part_at(m)].astype(f32)
        )
        if k:
            to_z[k - 1] = mine.astype(bf16)
            go(remote(to_z.at[k - 1], from_z.at[k - 1], Z3 + k - 1, member_id(k)))
        else:
            w_grad_ref[...] = mine

    lines = lines_of(grad_edges).astype(f32)
    taps = [moved(lines, 1 - s).astype(bf16) for s in range(3)]
    pieces = []
    for edge in range(4):
        piece = jnp.zeros((line, channels), f32)
        for s in range(3):
            dy, dx = ((0, s), (2, s), (s, 0), (s, 2))[edge]
            piece = piece + lax.dot_general(
                taps[s][edge * line : (edge + 1) * line],
                w_of(dy, dx),
                over_outputs,
                preferred_element_type=f32,
            )
        pieces.append(piece)
    cycle = jnp.concatenate(pieces, axis=0)
    high = cycle.astype(bf16)
    low = (cycle - high.astype(f32)).astype(bf16)
    q = lane_numbers(2 * line)
    lane_face, near = (q // size) % faces, q % size - row_start
    spot = lane_face * (band * size) + near * size + jnp.where(q < line, 0, size - 1)
    put = placing(jnp.where((near >= 0) & (near < band), spot, -1), cells)
    grad = grad.reshape(faces, band, size, channels)
    line_grad = jnp.zeros((4 * line, channels), f32)
    side_grad = jnp.zeros((cells, channels), f32)
    for level in (high, low):
        routed = jnp.dot(cross[...], level, preferred_element_type=f32)
        line_grad = line_grad + routed
        side_grad = side_grad + jnp.dot(
            put, routed[2 * line :].astype(bf16), preferred_element_type=f32
        )
    north = jnp.where(me == 0, line_grad[0:line], 0.0).reshape(faces, 1, size, channels)
    south = jnp.where(me == 3, line_grad[line : 2 * line], 0.0).reshape(faces, 1, size, channels)
    inner = jnp.zeros((faces, band - 2, size, channels), f32)
    grad = grad + jnp.concatenate([north, inner, south], axis=1)
    grad = grad.reshape(cells, channels) + side_grad
    in_grad_ref[...] = grad.astype(bf16)
    keep_grad = pltpu.make_async_copy(in_grad_ref, in_grad_hbm, load_sem.at[4])
    keep_grad.start()

    result = w_grad_ref[...]
    for k in range(1, 4):
        remote(from_z.at[k - 1], from_z.at[k - 1], Z3 + k - 1, member_id(k)).wait_recv()
        result = result + from_z[k - 1].astype(f32)
    w_grad_ref[...] = result * scale
    keep_w = pltpu.make_async_copy(w_grad_ref, w_grad_hbm, load_sem.at[5])
    keep_w.start()
    finish_edges(edges, EX)
    finish_edges(grad_edges, GX)
    for copy in started:
        copy.wait_send()
    keep_act.wait()
    keep_grad.wait()
    keep_w.wait()


def shards(fields, weight, cotangent, adjacency):
    members, faces, band, size, channels = fields.shape
    tiles, across = lax.axis_size("tile"), lax.axis_size("member")
    block = weight.shape[0]
    fits = tiles == 4 and across == 4 and members == 1 and band * tiles == size
    if not (fits and size == 16 and block % 16 == 0 and (faces * 2 * band) % 16 == 0):
        return plain_shards(fields, weight, cotangent, adjacency)
    cells = faces * band * size
    side, line = faces * 2 * band, faces * size
    bf16, f32 = jnp.bfloat16, jnp.float32
    scale = 1.0 / math.sqrt(cells * tiles * across)
    rows = block * tiles * across
    anywhere = pl.BlockSpec(memory_space=pl.ANY)
    results = pl.pallas_call(
        functools.partial(fused_kernel, (faces, band, size, channels), scale),
        out_shape=(
            jax.ShapeDtypeStruct((cells, channels), bf16),
            jax.ShapeDtypeStruct((cells, channels), bf16),
            jax.ShapeDtypeStruct((block, channels), f32),
        ),
        in_specs=[anywhere] * 3 + [pl.BlockSpec(memory_space=pltpu.SMEM)],
        out_specs=(anywhere,) * 3,
        scratch_shapes=[
            pltpu.VMEM((cells, channels), bf16),
            pltpu.VMEM((cells, channels), bf16),
            pltpu.VMEM((block, channels), f32),
            pltpu.VMEM((cells, channels), bf16),
            pltpu.VMEM((cells, channels), bf16),
            pltpu.VMEM((rows, channels), bf16),
            pltpu.VMEM((4, side + 2 * line, channels), bf16),
            pltpu.VMEM((4, side + 2 * line, channels), bf16),
            pltpu.VMEM((4 * line, 4 * line), bf16),
            pltpu.VMEM((3, faces, band + 2, size, channels), bf16),
            pltpu.VMEM((3, faces, band + 2, size, channels), bf16),
            pltpu.VMEM((rows, channels), f32),
            pltpu.VMEM((rows, channels), bf16),
            pltpu.VMEM((2, 4 * block, channels), bf16),
            pltpu.VMEM((4 * block, channels), bf16),
            pltpu.VMEM((4 * block, channels), bf16),
            pltpu.VMEM((3, block, channels), bf16),
            pltpu.VMEM((3, block, channels), bf16),
            pltpu.SemaphoreType.DMA((COPIES,)),
            pltpu.SemaphoreType.DMA((COPIES,)),
            pltpu.SemaphoreType.DMA((6,)),
        ],
        compiler_params=pltpu.CompilerParams(
            collective_id=0, has_side_effects=True, vmem_limit_bytes=60 * 1024 * 1024
        ),
    )(
        fields.reshape(cells, channels),
        weight,
        cotangent.reshape(cells, channels),
        adjacency.transpose(2, 1, 0),
    )
    act, in_grad, w_grad = pl.pallas_call(
        store_kernel,
        out_shape=tuple(jax.ShapeDtypeStruct(r.shape, r.dtype) for r in results),
        in_specs=[anywhere] * 3,
        out_specs=(anywhere,) * 3,
        scratch_shapes=[pltpu.SemaphoreType.DMA((3,))],
        compiler_params=pltpu.CompilerParams(vmem_limit_bytes=60 * 1024 * 1024),
    )(*results)
    return act.reshape(fields.shape), in_grad.reshape(fields.shape), w_grad


def solution(mesh):
    in_specs = (
        P(("groups", "member"), None, "tile", None, None),
        P(("tile", "member"), None),
        P(("groups", "member"), None, "tile", None, None),
        P(),
    )
    out_specs = (
        P(("groups", "member"), None, "tile", None, None),
        P(("groups", "member"), None, "tile", None, None),
        P(("groups", "tile", "member"), None),
    )
    return jax.shard_map(shards, mesh=mesh, in_specs=in_specs, out_specs=out_specs, check_vma=False)
```

```python
import functools
import math

import jax
import jax.numpy as jnp
from jax import lax
from jax.experimental import pallas as pl
from jax.experimental.pallas import tpu as pltpu
from jax.sharding import PartitionSpec as P

gelu_scale = 0.7978845608028654


def from_root(value, axis, source):
    kept = jnp.where(lax.axis_index(axis) == source, value, 0).astype(value.dtype)
    return lax.psum(kept, axis)


def extended(cells, sides, width):
    for axis, dim in sides:
        count = lax.axis_size(axis)
        ends = count - 1
        head = lax.slice_in_dim(cells, 0, width, axis=dim)
        tail = lax.slice_in_dim(cells, cells.shape[dim] - width, cells.shape[dim], axis=dim)
        cells = jnp.concatenate(
            [
                lax.ppermute(tail, axis, [(i, (i + 1) % count) for i in range(ends)]),
                cells,
                lax.ppermute(head, axis, [((i + 1) % count, i) for i in range(ends)]),
            ],
            axis=dim,
        )
    return cells


def gelu_tanh(argument):
    return (
        0.5
        * argument
        * (1.0 + jnp.tanh(gelu_scale * (argument + 0.044715 * argument * argument * argument)))
    )


def edge_selector(adjacency):
    source_index = adjacency[:, :, 2] * 24 + adjacency[:, :, 0] * 4 + adjacency[:, :, 1]
    source_index = source_index.reshape(24)
    return (source_index[:, None] == jnp.arange(48, dtype=jnp.int32)[None, :]).astype(jnp.float32)


def route_lines(cycle_grad, selector):
    members, face_count, edges, face_size, channels = cycle_grad.shape
    flat_cycle = cycle_grad.reshape(members, 24, face_size, channels)
    routed = jnp.einsum("ts,mtfc->msfc", selector, flat_cycle, precision=lax.Precision.HIGHEST)
    line_grad = routed[:, :24] + routed[:, 24:, ::-1]
    return line_grad.reshape(members, face_count, 4, face_size, channels)


def plain_shards(fields, weight, cotangent, adjacency):
    members, face_count, band_rows, face_size, channels = fields.shape
    position = lax.axis_index("tile")
    tile_count = lax.axis_size("tile")
    top_device = position == 0
    bottom_device = position == tile_count - 1
    row_start = position * band_rows
    selector = edge_selector(adjacency)
    full_weight = lax.all_gather(weight, ("tile", "member"), axis=0, tiled=True)
    side_columns = jnp.stack([fields[:, :, :, 0, :], fields[:, :, :, -1, :]], axis=2)
    all_columns = lax.all_gather(side_columns, "tile", axis=3, tiled=True)
    north_lines = from_root(fields[:, :, 0, :, :], "tile", 0)
    south_lines = from_root(fields[:, :, -1, :, :], "tile", tile_count - 1)
    edge_lines = jnp.concatenate(
        [north_lines[:, :, None], south_lines[:, :, None], all_columns], axis=2
    )
    edge_lines = edge_lines.reshape(members, 24, face_size, channels)
    both_ways = jnp.concatenate([edge_lines, edge_lines[:, :, ::-1]], axis=1)
    cycle_cells = jnp.einsum(
        "ts,msfc->mtfc",
        selector.astype(jnp.bfloat16),
        both_ways,
        preferred_element_type=jnp.float32,
    )
    cycle_cells = cycle_cells.astype(jnp.bfloat16).reshape(
        members, face_count, 4, face_size, channels
    )
    side_cycle = lax.dynamic_slice_in_dim(cycle_cells[:, :, 2:4], row_start, band_rows, 3)
    widened = jnp.concatenate(
        [side_cycle[:, :, 0][:, :, :, None], fields, side_cycle[:, :, 1][:, :, :, None]], axis=3
    )
    padded = extended(widened, (("tile", 2),), 1)
    zero_cell = jnp.zeros((members, face_count, 1, channels), jnp.bfloat16)
    north_row = jnp.concatenate([zero_cell, cycle_cells[:, :, 0], zero_cell], axis=2)
    south_row = jnp.concatenate([zero_cell, cycle_cells[:, :, 1], zero_cell], axis=2)
    padded = padded.at[:, :, 0].set(jnp.where(top_device, north_row, padded[:, :, 0]))
    padded = padded.at[:, :, -1].set(jnp.where(bottom_device, south_row, padded[:, :, -1]))
    cell_count = members * face_count * band_rows * face_size
    pre_act = jnp.zeros((cell_count, channels), jnp.float32)
    for row_step in range(3):
        for col_step in range(3):
            offset = 3 * row_step + col_step
            window = padded[
                :, :, row_step : row_step + band_rows, col_step : col_step + face_size
            ].reshape(cell_count, channels)
            pre_act = pre_act + jnp.dot(
                window,
                full_weight[offset * channels : (offset + 1) * channels],
                preferred_element_type=jnp.float32,
            )
    activation = gelu_tanh(pre_act).astype(jnp.bfloat16).reshape(fields.shape)
    unused_value, pullback = jax.vjp(gelu_tanh, pre_act)
    act_grad = pullback(cotangent.reshape(cell_count, channels).astype(jnp.float32))[0].astype(
        jnp.bfloat16
    )
    grad_terms = []
    grad_pad = jnp.zeros((members, face_count, band_rows + 2, face_size + 2, channels), jnp.float32)
    for row_step in range(3):
        for col_step in range(3):
            offset = 3 * row_step + col_step
            window = padded[
                :, :, row_step : row_step + band_rows, col_step : col_step + face_size
            ].reshape(cell_count, channels)
            grad_terms.append(
                lax.dot_general(
                    window, act_grad, (((0,), (0,)), ((), ())), preferred_element_type=jnp.float32
                )
            )
            kernel_rows = full_weight[offset * channels : (offset + 1) * channels]
            product_term = jnp.dot(act_grad, kernel_rows.T, preferred_element_type=jnp.float32)
            product_term = product_term.reshape(members, face_count, band_rows, face_size, channels)
            grad_pad = grad_pad.at[
                :, :, row_step : row_step + band_rows, col_step : col_step + face_size
            ].add(product_term)
    local_grad = jnp.concatenate(grad_terms, axis=0)
    owned_rows = lax.psum_scatter(local_grad, ("tile", "member"), scatter_dimension=0, tiled=True)
    total_cells = cell_count * tile_count * lax.axis_size("member")
    weight_grad = owned_rows / math.sqrt(total_cells)
    cycle_rows = jnp.stack([grad_pad[:, :, 0], grad_pad[:, :, -1]], axis=2)
    received = extended(cycle_rows, (("tile", 2),), 1)
    band_grad = grad_pad[:, :, 1:-1]
    band_grad = band_grad.at[:, :, 0].add(received[:, :, 0])
    band_grad = band_grad.at[:, :, -1].add(received[:, :, 3])
    side_grad = jnp.stack([band_grad[:, :, :, 0], band_grad[:, :, :, -1]], axis=2)
    side_full = lax.dynamic_update_slice_in_dim(
        jnp.zeros((members, face_count, 2, face_size, channels), jnp.float32),
        side_grad,
        row_start,
        3,
    )
    north_grad = jnp.where(top_device, grad_pad[:, :, 0, 1:-1], 0.0)
    south_grad = jnp.where(bottom_device, grad_pad[:, :, -1, 1:-1], 0.0)
    cycle_grad = jnp.concatenate(
        [north_grad[:, :, None], south_grad[:, :, None], side_full], axis=2
    )
    line_grad = route_lines(cycle_grad, selector)
    side_share = lax.psum_scatter(
        line_grad[:, :, 2:4].astype(jnp.bfloat16), "tile", scatter_dimension=3, tiled=True
    ).astype(jnp.float32)
    top_bottom = lax.psum(line_grad[:, :, 0:2].astype(jnp.bfloat16), "tile").astype(jnp.float32)
    cell_grad = band_grad[:, :, :, 1:-1]
    cell_grad = cell_grad.at[:, :, :, 0].add(side_share[:, :, 0])
    cell_grad = cell_grad.at[:, :, :, -1].add(side_share[:, :, 1])
    cell_grad = cell_grad.at[:, :, 0].add(jnp.where(top_device, top_bottom[:, :, 0], 0.0))
    cell_grad = cell_grad.at[:, :, -1].add(jnp.where(bottom_device, top_bottom[:, :, 1], 0.0))
    input_grad = cell_grad.astype(jnp.bfloat16)
    return (activation, input_grad, weight_grad)


MESH = pl.DeviceIdType.MESH
COPIES = 45
WZ, WX, WS, WD, EX, GX, R1, X2, Z3 = 0, 3, 7, 11, 15, 24, 33, 38, 42


def lane_numbers(width):
    return lax.broadcasted_iota(jnp.int32, (1, width), 1)


def placing(row_of_lane, rows):
    width = row_of_lane.shape[1]
    numbers = lax.broadcasted_iota(jnp.int32, (rows, width), 0)
    return jnp.where(numbers == row_of_lane, 1.0, 0.0).astype(jnp.bfloat16)


def store_kernel(*refs):
    sources, targets, staged, sems = refs[0:3], refs[3:6], refs[6:9], refs[9]
    loads = [pltpu.make_async_copy(sources[i], staged[i], sems.at[i]) for i in range(3)]
    stores = [pltpu.make_async_copy(staged[i], targets[i], sems.at[3 + i]) for i in range(3)]
    for load in loads:
        load.start()
    for load, store in zip(loads, stores):
        load.wait()
        store.start()
    for store in stores:
        store.wait()


def fused_kernel(
    dims,
    scale,
    fields_hbm,
    weight_hbm,
    cot_hbm,
    adjacency_ref,
    act_hbm,
    in_grad_hbm,
    w_grad_hbm,
    act_ref,
    in_grad_ref,
    w_grad_ref,
    fields_ref,
    cot_ref,
    full_w,
    edges,
    grad_edges,
    cross,
    padded,
    shifted,
    total,
    outgoing,
    from_core,
    to_x,
    from_x,
    to_z,
    from_z,
    send_sem,
    recv_sem,
    load_sem,
):
    faces, band, size, channels = dims
    cells = faces * band * size
    line = faces * size
    side = faces * 2 * band
    block = weight_hbm.shape[0]
    quarter = 4 * block
    f32, bf16 = jnp.float32, jnp.bfloat16
    me = lax.axis_index("tile")
    z = lax.axis_index("member")
    chip, core = me // 2, me % 2
    sib = chip * 2 + (1 - core)
    across = (1 - chip) * 2 + core
    diag = (1 - chip) * 2 + (1 - core)
    tile_peers = (sib, across, diag)

    def remote(src, dst, sem, target):
        return pltpu.make_async_remote_copy(
            src_ref=src,
            dst_ref=dst,
            send_sem=send_sem.at[sem],
            recv_sem=recv_sem.at[sem],
            device_id=target,
            device_id_type=MESH,
        )

    def tile_id(t):
        return {"tile": t}

    def member_id(k):
        return {"member": (z + k) % 4}

    def w_block(t, m):
        return full_w.at[pl.ds(pl.multiple_of((t * 4 + m) * block, 16), block)]

    def edge_parts(buf, first, source, target):
        top = (source == 0) | (target == source - 1)
        bottom = (source == 3) | (target == source + 1)
        spans = ((0, side, None), (side, line, top), (side + line, line, bottom))
        for part, (start, count, needed) in enumerate(spans):
            piece = buf.at[source, pl.ds(start, count)]
            yield needed, piece, first + part

    def when(needed, action):
        if needed is None:
            action()
        else:
            pl.when(needed)(action)

    def each_edge(buf, first, incoming, action):
        for k, t in enumerate(tile_peers):
            source, target = (t, me) if incoming else (me, t)
            for needed, piece, sem in edge_parts(buf, first + 3 * k, source, target):
                when(needed, functools.partial(action, remote(piece, piece, sem, tile_id(t))))

    def send_edges(buf, first):
        each_edge(buf, first, False, lambda copy: copy.start())

    def take_edges(buf, first):
        each_edge(buf, first, True, lambda copy: copy.wait_recv())

    def finish_edges(buf, first):
        each_edge(buf, first, False, lambda copy: copy.wait_send())

    load_w = pltpu.make_async_copy(weight_hbm, w_block(me, z), load_sem.at[0])
    load_fields = pltpu.make_async_copy(fields_hbm, fields_ref, load_sem.at[1])
    load_cot = pltpu.make_async_copy(cot_hbm, cot_ref, load_sem.at[2])
    for load in (load_w, load_fields, load_cot):
        load.start()

    barrier = pltpu.get_barrier_semaphore()
    for t in tile_peers:
        pl.semaphore_signal(barrier, inc=1, device_id=tile_id(t), device_id_type=MESH)
    for k in range(1, 4):
        pl.semaphore_signal(barrier, inc=1, device_id=member_id(k), device_id_type=MESH)

    row_start = me * band
    q = lane_numbers(cells)
    col, row, face = q % size, (q // size) % band, q // (size * band)
    target = face * (2 * band) + row + jnp.where(col == 0, 0, band)
    side_pick = placing(jnp.where((col == 0) | (col == size - 1), target, -1), side)

    def own_edges(values, out):
        cube = values.reshape(faces, band, size, channels)
        out[me, 0:side] = jnp.dot(side_pick, values, preferred_element_type=f32).astype(bf16)
        out[me, side : side + line] = cube[:, 0].reshape(line, channels)
        out[me, side + line : side + 2 * line] = cube[:, band - 1].reshape(line, channels)

    load_w.wait()
    pl.semaphore_wait(barrier, 6)

    started = []

    def go(copy):
        copy.start()
        started.append(copy)

    for k in (2, 1, 3):
        go(remote(w_block(me, z), w_block(me, z), WZ + k - 1, member_id(k)))
    load_fields.wait()
    own_edges(fields_ref[...], edges)
    send_edges(edges, EX)

    def w_spread(k):
        part = w_block(me, (z + 4 - k) % 4)
        if k:
            remote(part, part, WZ + k - 1, member_id(k)).wait_recv()
        go(remote(part, part, WX + k, tile_id(across)))
        go(remote(part, part, WS + k, tile_id(sib)))

    w_spread(0)
    q = lane_numbers(4 * line)
    bank, along = q // size, q % size
    base, turned = jnp.zeros_like(q), jnp.zeros_like(q)
    for f in range(faces):
        for e in range(4):
            here = bank == e * faces + f
            start = adjacency_ref[1, e, f] * line + adjacency_ref[0, e, f] * size
            base = jnp.where(here, start, base)
            turned = jnp.where(here, adjacency_ref[2, e, f], turned)
    cross[...] = placing(base + along + turned * (size - 1 - 2 * along), 4 * line)
    q = lane_numbers(4 * side)
    band_of, rest = q // side, q % side
    order = placing(
        ((rest // band) % 2) * line
        + (rest // (2 * band)) * size
        + band_of * band
        + rest % band,
        2 * line,
    )
    for k in (1, 3, 2):
        w_spread(k)

    def columns(rows):
        return lax.broadcasted_iota(jnp.int32, (rows, 1), 0) % size

    def moved(values, step):
        rows = values.shape[0]
        if step == 0:
            return values
        if step < 0:
            return jnp.where(columns(rows) == 0, 0.0, pltpu.roll(values, 1, 0))
        return jnp.where(columns(rows) == size - 1, 0.0, pltpu.roll(values, rows - 1, 0))

    def with_halo(values, buf, north, south):
        above = buf[jnp.maximum(me - 1, 0), side + line : side + 2 * line].astype(f32)
        below = buf[jnp.minimum(me + 1, 3), side : side + line].astype(f32)
        above = jnp.where(me > 0, above, north).reshape(faces, 1, size, channels)
        below = jnp.where(me < 3, below, south).reshape(faces, 1, size, channels)
        own = values.astype(f32).reshape(faces, band, size, channels)
        return jnp.concatenate([above, own, below], axis=1).reshape(-1, channels)

    def lines_of(buf):
        sides = jnp.concatenate([buf[t, 0:side] for t in range(4)], axis=0)
        sides = jnp.dot(order, sides, preferred_element_type=f32).astype(bf16)
        north = buf[0, side : side + line]
        south = buf[3, side + line : side + 2 * line]
        return jnp.concatenate([north, south, sides], axis=0)

    take_edges(edges, EX)
    cycle_cells = jnp.dot(cross[...], lines_of(edges), preferred_element_type=f32)
    center = with_halo(
        fields_ref[...], edges, cycle_cells[0:line], cycle_cells[line : 2 * line]
    )
    cycle_sides = cycle_cells[2 * line :].astype(bf16)
    q = lane_numbers(line)
    near = q % size - row_start + 1
    spot = (q // size) * ((band + 2) * size) + near * size
    inside = (near >= 0) & (near < band + 2)
    for dx in range(3):
        values = moved(center, dx - 1)
        if dx != 1:
            first = line if dx else 0
            put = placing(
                jnp.where(inside, spot + (size - 1 if dx else 0), -1), faces * (band + 2) * size
            )
            values = values + jnp.dot(
                put, cycle_sides[first : first + line], preferred_element_type=f32
            )
        padded[dx] = values.astype(bf16).reshape(faces, band + 2, size, channels)

    for k in (0, 1, 3, 2):
        part = w_block(across, (z + 4 - k) % 4)
        remote(part, part, WX + k, tile_id(across)).wait_recv()
        go(remote(part, part, WD + k, tile_id(sib)))
    for k in range(4):
        part = w_block(sib, (z + 4 - k) % 4)
        remote(part, part, WS + k, tile_id(sib)).wait_recv()
        part = w_block(diag, (z + 4 - k) % 4)
        remote(part, part, WD + k, tile_id(sib)).wait_recv()

    def window(dy, dx):
        return padded[dx, :, dy : dy + band].reshape(cells, channels)

    def w_of(dy, dx):
        first = (3 * dy + dx) * channels
        return full_w[first : first + channels]

    pre = jnp.zeros((cells, channels), f32)
    for dy in range(3):
        for dx in range(3):
            pre = pre + jnp.dot(window(dy, dx), w_of(dy, dx), preferred_element_type=f32)
    load_cot.wait()
    square = pre * pre
    bend = jnp.tanh(gelu_scale * (pre + 0.044715 * pre * square))
    act_ref[...] = (0.5 * pre * (1.0 + bend)).astype(bf16)
    keep_act = pltpu.make_async_copy(act_ref, act_hbm, load_sem.at[3])
    keep_act.start()
    slope = 0.5 * (1.0 + bend) + 0.5 * pre * (1.0 - bend * bend) * (
        gelu_scale * (1.0 + 3 * 0.044715 * square)
    )
    act_grad = (cot_ref[...].astype(f32) * slope).astype(bf16)
    own_edges(act_grad, grad_edges)
    send_edges(grad_edges, GX)

    for dy in range(3):
        for dx in range(3):
            first = (3 * dy + dx) * channels
            part = lax.dot_general(
                window(dy, dx), act_grad, (((0,), (0,)), ((), ())), preferred_element_type=f32
            )
            total[first : first + channels] = part
            outgoing[first : first + channels] = part.astype(bf16)

    def quarter_at(t):
        return pl.ds(pl.multiple_of(t * quarter, 16), quarter)

    def part_at(m):
        return pl.ds(pl.multiple_of(m * block, 16), block)

    def row_at(t, m):
        return pl.ds(pl.multiple_of((t * 4 + m) * block, 16), block)

    for k in (2, 1, 3, 0):
        m = (z + k) % 4
        there = from_core.at[0, part_at(m)]
        go(remote(outgoing.at[row_at(diag, m)], there, R1 + k, tile_id(sib)))
    go(remote(outgoing.at[quarter_at(sib)], from_core.at[1], R1 + 4, tile_id(sib)))

    for k in (2, 1, 3, 0):
        m = (z + k) % 4
        there = from_core.at[0, part_at(m)]
        remote(there, there, R1 + k, tile_id(sib)).wait_recv()
        to_x[part_at(m)] = (
            total[row_at(across, m)] + from_core[0, part_at(m)].astype(f32)
        ).astype(bf16)
        go(remote(to_x.at[part_at(m)], from_x.at[part_at(m)], X2 + k, tile_id(across)))

    take_edges(grad_edges, GX)
    center = with_halo(act_grad, grad_edges, 0.0, 0.0)
    for dx in range(3):
        shifted[dx] = (
            moved(center, 1 - dx).astype(bf16).reshape(faces, band + 2, size, channels)
        )
    grad = jnp.zeros((cells, channels), f32)
    over_outputs = (((1,), (1,)), ((), ()))
    for dy in range(3):
        for dx in range(3):
            grad = grad + lax.dot_general(
                shifted[dx, :, 2 - dy : 2 - dy + band].reshape(cells, channels),
                w_of(dy, dx),
                over_outputs,
                preferred_element_type=f32,
            )

    remote(from_core.at[1], from_core.at[1], R1 + 4, tile_id(sib)).wait_recv()
    for k in (2, 1, 3, 0):
        m = (z + k) % 4
        remote(to_x.at[part_at(m)], from_x.at[part_at(m)], X2 + k, tile_id(across)).wait_recv()
        mine = (
            total[row_at(me, m)]
            + from_core[1, part_at(m)].astype(f32)
            + from_x[part_at(m)].astype(f32)
        )
        if k:
            to_z[k - 1] = mine.astype(bf16)
            go(remote(to_z.at[k - 1], from_z.at[k - 1], Z3 + k - 1, member_id(k)))
        else:
            w_grad_ref[...] = mine

    lines = lines_of(grad_edges).astype(f32)
    taps = [moved(lines, 1 - s).astype(bf16) for s in range(3)]
    pieces = []
    for edge in range(4):
        piece = jnp.zeros((line, channels), f32)
        for s in range(3):
            dy, dx = ((0, s), (2, s), (s, 0), (s, 2))[edge]
            piece = piece + lax.dot_general(
                taps[s][edge * line : (edge + 1) * line],
                w_of(dy, dx),
                over_outputs,
                preferred_element_type=f32,
            )
        pieces.append(piece)
    cycle = jnp.concatenate(pieces, axis=0)
    high = cycle.astype(bf16)
    low = (cycle - high.astype(f32)).astype(bf16)
    q = lane_numbers(2 * line)
    lane_face, near = (q // size) % faces, q % size - row_start
    spot = lane_face * (band * size) + near * size + jnp.where(q < line, 0, size - 1)
    put = placing(jnp.where((near >= 0) & (near < band), spot, -1), cells)
    grad = grad.reshape(faces, band, size, channels)
    line_grad = jnp.zeros((4 * line, channels), f32)
    side_grad = jnp.zeros((cells, channels), f32)
    for level in (high, low):
        routed = jnp.dot(cross[...], level, preferred_element_type=f32)
        line_grad = line_grad + routed
        side_grad = side_grad + jnp.dot(
            put, routed[2 * line :].astype(bf16), preferred_element_type=f32
        )
    north = jnp.where(me == 0, line_grad[0:line], 0.0).reshape(faces, 1, size, channels)
    south = jnp.where(me == 3, line_grad[line : 2 * line], 0.0).reshape(faces, 1, size, channels)
    inner = jnp.zeros((faces, band - 2, size, channels), f32)
    grad = grad + jnp.concatenate([north, inner, south], axis=1)
    grad = grad.reshape(cells, channels) + side_grad
    in_grad_ref[...] = grad.astype(bf16)
    keep_grad = pltpu.make_async_copy(in_grad_ref, in_grad_hbm, load_sem.at[4])
    keep_grad.start()

    result = w_grad_ref[...]
    for k in range(1, 4):
        remote(from_z.at[k - 1], from_z.at[k - 1], Z3 + k - 1, member_id(k)).wait_recv()
        result = result + from_z[k - 1].astype(f32)
    w_grad_ref[...] = result * scale
    keep_w = pltpu.make_async_copy(w_grad_ref, w_grad_hbm, load_sem.at[5])
    keep_w.start()
    finish_edges(edges, EX)
    finish_edges(grad_edges, GX)
    for copy in started:
        copy.wait_send()
    keep_act.wait()
    keep_grad.wait()
    keep_w.wait()


def shards(fields, weight, cotangent, adjacency):
    members, faces, band, size, channels = fields.shape
    tiles, across = lax.axis_size("tile"), lax.axis_size("member")
    block = weight.shape[0]
    fits = tiles == 4 and across == 4 and members == 1 and band * tiles == size
    if not (fits and size == 16 and block % 16 == 0 and (faces * 2 * band) % 16 == 0):
        return plain_shards(fields, weight, cotangent, adjacency)
    cells = faces * band * size
    side, line = faces * 2 * band, faces * size
    bf16, f32 = jnp.bfloat16, jnp.float32
    scale = 1.0 / math.sqrt(cells * tiles * across)
    rows = block * tiles * across
    anywhere = pl.BlockSpec(memory_space=pl.ANY)
    results = pl.pallas_call(
        functools.partial(fused_kernel, (faces, band, size, channels), scale),
        out_shape=(
            jax.ShapeDtypeStruct((cells, channels), bf16),
            jax.ShapeDtypeStruct((cells, channels), bf16),
            jax.ShapeDtypeStruct((block, channels), f32),
        ),
        in_specs=[anywhere] * 3 + [pl.BlockSpec(memory_space=pltpu.SMEM)],
        out_specs=(anywhere,) * 3,
        scratch_shapes=[
            pltpu.VMEM((cells, channels), bf16),
            pltpu.VMEM((cells, channels), bf16),
            pltpu.VMEM((block, channels), f32),
            pltpu.VMEM((cells, channels), bf16),
            pltpu.VMEM((cells, channels), bf16),
            pltpu.VMEM((rows, channels), bf16),
            pltpu.VMEM((4, side + 2 * line, channels), bf16),
            pltpu.VMEM((4, side + 2 * line, channels), bf16),
            pltpu.VMEM((4 * line, 4 * line), bf16),
            pltpu.VMEM((3, faces, band + 2, size, channels), bf16),
            pltpu.VMEM((3, faces, band + 2, size, channels), bf16),
            pltpu.VMEM((rows, channels), f32),
            pltpu.VMEM((rows, channels), bf16),
            pltpu.VMEM((2, 4 * block, channels), bf16),
            pltpu.VMEM((4 * block, channels), bf16),
            pltpu.VMEM((4 * block, channels), bf16),
            pltpu.VMEM((3, block, channels), bf16),
            pltpu.VMEM((3, block, channels), bf16),
            pltpu.SemaphoreType.DMA((COPIES,)),
            pltpu.SemaphoreType.DMA((COPIES,)),
            pltpu.SemaphoreType.DMA((6,)),
        ],
        compiler_params=pltpu.CompilerParams(
            collective_id=0, has_side_effects=True, vmem_limit_bytes=60 * 1024 * 1024
        ),
    )(
        fields.reshape(cells, channels),
        weight,
        cotangent.reshape(cells, channels),
        adjacency.transpose(2, 1, 0),
    )
    act, in_grad, w_grad = pl.pallas_call(
        store_kernel,
        out_shape=tuple(jax.ShapeDtypeStruct(r.shape, r.dtype) for r in results),
        in_specs=[anywhere] * 3,
        out_specs=(anywhere,) * 3,
        scratch_shapes=[pltpu.VMEM(r.shape, r.dtype) for r in results]
        + [pltpu.SemaphoreType.DMA((6,))],
        compiler_params=pltpu.CompilerParams(vmem_limit_bytes=60 * 1024 * 1024),
    )(*results)
    return act.reshape(fields.shape), in_grad.reshape(fields.shape), w_grad


def solution(mesh):
    in_specs = (
        P(("groups", "member"), None, "tile", None, None),
        P(("tile", "member"), None),
        P(("groups", "member"), None, "tile", None, None),
        P(),
    )
    out_specs = (
        P(("groups", "member"), None, "tile", None, None),
        P(("groups", "member"), None, "tile", None, None),
        P(("groups", "tile", "member"), None),
    )
    return jax.shard_map(shards, mesh=mesh, in_specs=in_specs, out_specs=out_specs, check_vma=False)
```

```python
import functools
import math

import jax
import jax.numpy as jnp
from jax import lax
from jax.experimental import pallas as pl
from jax.experimental.pallas import tpu as pltpu
from jax.sharding import PartitionSpec as P

gelu_scale = 0.7978845608028654


def from_root(value, axis, source):
    kept = jnp.where(lax.axis_index(axis) == source, value, 0).astype(value.dtype)
    return lax.psum(kept, axis)


def extended(cells, sides, width):
    for axis, dim in sides:
        count = lax.axis_size(axis)
        ends = count - 1
        head = lax.slice_in_dim(cells, 0, width, axis=dim)
        tail = lax.slice_in_dim(cells, cells.shape[dim] - width, cells.shape[dim], axis=dim)
        cells = jnp.concatenate(
            [
                lax.ppermute(tail, axis, [(i, (i + 1) % count) for i in range(ends)]),
                cells,
                lax.ppermute(head, axis, [((i + 1) % count, i) for i in range(ends)]),
            ],
            axis=dim,
        )
    return cells


def gelu_tanh(argument):
    return (
        0.5
        * argument
        * (1.0 + jnp.tanh(gelu_scale * (argument + 0.044715 * argument * argument * argument)))
    )


def edge_selector(adjacency):
    source_index = adjacency[:, :, 2] * 24 + adjacency[:, :, 0] * 4 + adjacency[:, :, 1]
    source_index = source_index.reshape(24)
    return (source_index[:, None] == jnp.arange(48, dtype=jnp.int32)[None, :]).astype(jnp.float32)


def route_lines(cycle_grad, selector):
    members, face_count, edges, face_size, channels = cycle_grad.shape
    flat_cycle = cycle_grad.reshape(members, 24, face_size, channels)
    routed = jnp.einsum("ts,mtfc->msfc", selector, flat_cycle, precision=lax.Precision.HIGHEST)
    line_grad = routed[:, :24] + routed[:, 24:, ::-1]
    return line_grad.reshape(members, face_count, 4, face_size, channels)


def plain_shards(fields, weight, cotangent, adjacency):
    members, face_count, band_rows, face_size, channels = fields.shape
    position = lax.axis_index("tile")
    tile_count = lax.axis_size("tile")
    top_device = position == 0
    bottom_device = position == tile_count - 1
    row_start = position * band_rows
    selector = edge_selector(adjacency)
    full_weight = lax.all_gather(weight, ("tile", "member"), axis=0, tiled=True)
    side_columns = jnp.stack([fields[:, :, :, 0, :], fields[:, :, :, -1, :]], axis=2)
    all_columns = lax.all_gather(side_columns, "tile", axis=3, tiled=True)
    north_lines = from_root(fields[:, :, 0, :, :], "tile", 0)
    south_lines = from_root(fields[:, :, -1, :, :], "tile", tile_count - 1)
    edge_lines = jnp.concatenate(
        [north_lines[:, :, None], south_lines[:, :, None], all_columns], axis=2
    )
    edge_lines = edge_lines.reshape(members, 24, face_size, channels)
    both_ways = jnp.concatenate([edge_lines, edge_lines[:, :, ::-1]], axis=1)
    cycle_cells = jnp.einsum(
        "ts,msfc->mtfc",
        selector.astype(jnp.bfloat16),
        both_ways,
        preferred_element_type=jnp.float32,
    )
    cycle_cells = cycle_cells.astype(jnp.bfloat16).reshape(
        members, face_count, 4, face_size, channels
    )
    side_cycle = lax.dynamic_slice_in_dim(cycle_cells[:, :, 2:4], row_start, band_rows, 3)
    widened = jnp.concatenate(
        [side_cycle[:, :, 0][:, :, :, None], fields, side_cycle[:, :, 1][:, :, :, None]], axis=3
    )
    padded = extended(widened, (("tile", 2),), 1)
    zero_cell = jnp.zeros((members, face_count, 1, channels), jnp.bfloat16)
    north_row = jnp.concatenate([zero_cell, cycle_cells[:, :, 0], zero_cell], axis=2)
    south_row = jnp.concatenate([zero_cell, cycle_cells[:, :, 1], zero_cell], axis=2)
    padded = padded.at[:, :, 0].set(jnp.where(top_device, north_row, padded[:, :, 0]))
    padded = padded.at[:, :, -1].set(jnp.where(bottom_device, south_row, padded[:, :, -1]))
    cell_count = members * face_count * band_rows * face_size
    pre_act = jnp.zeros((cell_count, channels), jnp.float32)
    for row_step in range(3):
        for col_step in range(3):
            offset = 3 * row_step + col_step
            window = padded[
                :, :, row_step : row_step + band_rows, col_step : col_step + face_size
            ].reshape(cell_count, channels)
            pre_act = pre_act + jnp.dot(
                window,
                full_weight[offset * channels : (offset + 1) * channels],
                preferred_element_type=jnp.float32,
            )
    activation = gelu_tanh(pre_act).astype(jnp.bfloat16).reshape(fields.shape)
    unused_value, pullback = jax.vjp(gelu_tanh, pre_act)
    act_grad = pullback(cotangent.reshape(cell_count, channels).astype(jnp.float32))[0].astype(
        jnp.bfloat16
    )
    grad_terms = []
    grad_pad = jnp.zeros((members, face_count, band_rows + 2, face_size + 2, channels), jnp.float32)
    for row_step in range(3):
        for col_step in range(3):
            offset = 3 * row_step + col_step
            window = padded[
                :, :, row_step : row_step + band_rows, col_step : col_step + face_size
            ].reshape(cell_count, channels)
            grad_terms.append(
                lax.dot_general(
                    window, act_grad, (((0,), (0,)), ((), ())), preferred_element_type=jnp.float32
                )
            )
            kernel_rows = full_weight[offset * channels : (offset + 1) * channels]
            product_term = jnp.dot(act_grad, kernel_rows.T, preferred_element_type=jnp.float32)
            product_term = product_term.reshape(members, face_count, band_rows, face_size, channels)
            grad_pad = grad_pad.at[
                :, :, row_step : row_step + band_rows, col_step : col_step + face_size
            ].add(product_term)
    local_grad = jnp.concatenate(grad_terms, axis=0)
    owned_rows = lax.psum_scatter(local_grad, ("tile", "member"), scatter_dimension=0, tiled=True)
    total_cells = cell_count * tile_count * lax.axis_size("member")
    weight_grad = owned_rows / math.sqrt(total_cells)
    cycle_rows = jnp.stack([grad_pad[:, :, 0], grad_pad[:, :, -1]], axis=2)
    received = extended(cycle_rows, (("tile", 2),), 1)
    band_grad = grad_pad[:, :, 1:-1]
    band_grad = band_grad.at[:, :, 0].add(received[:, :, 0])
    band_grad = band_grad.at[:, :, -1].add(received[:, :, 3])
    side_grad = jnp.stack([band_grad[:, :, :, 0], band_grad[:, :, :, -1]], axis=2)
    side_full = lax.dynamic_update_slice_in_dim(
        jnp.zeros((members, face_count, 2, face_size, channels), jnp.float32),
        side_grad,
        row_start,
        3,
    )
    north_grad = jnp.where(top_device, grad_pad[:, :, 0, 1:-1], 0.0)
    south_grad = jnp.where(bottom_device, grad_pad[:, :, -1, 1:-1], 0.0)
    cycle_grad = jnp.concatenate(
        [north_grad[:, :, None], south_grad[:, :, None], side_full], axis=2
    )
    line_grad = route_lines(cycle_grad, selector)
    side_share = lax.psum_scatter(
        line_grad[:, :, 2:4].astype(jnp.bfloat16), "tile", scatter_dimension=3, tiled=True
    ).astype(jnp.float32)
    top_bottom = lax.psum(line_grad[:, :, 0:2].astype(jnp.bfloat16), "tile").astype(jnp.float32)
    cell_grad = band_grad[:, :, :, 1:-1]
    cell_grad = cell_grad.at[:, :, :, 0].add(side_share[:, :, 0])
    cell_grad = cell_grad.at[:, :, :, -1].add(side_share[:, :, 1])
    cell_grad = cell_grad.at[:, :, 0].add(jnp.where(top_device, top_bottom[:, :, 0], 0.0))
    cell_grad = cell_grad.at[:, :, -1].add(jnp.where(bottom_device, top_bottom[:, :, 1], 0.0))
    input_grad = cell_grad.astype(jnp.bfloat16)
    return (activation, input_grad, weight_grad)


MESH = pl.DeviceIdType.MESH
COPIES = 45
WZ, WX, WS, WD, EX, GX, R1, X2, Z3 = 0, 3, 7, 11, 15, 24, 33, 38, 42


def lane_numbers(width):
    return lax.broadcasted_iota(jnp.int32, (1, width), 1)


def placing(row_of_lane, rows):
    width = row_of_lane.shape[1]
    numbers = lax.broadcasted_iota(jnp.int32, (rows, width), 0)
    return jnp.where(numbers == row_of_lane, 1.0, 0.0).astype(jnp.bfloat16)


def store_kernel(*refs):
    sources, targets, staged, sems = refs[0:3], refs[3:6], refs[6:9], refs[9]
    loads = [pltpu.make_async_copy(sources[i], staged[i], sems.at[i]) for i in range(3)]
    stores = [pltpu.make_async_copy(staged[i], targets[i], sems.at[3 + i]) for i in range(3)]
    for load in loads:
        load.start()
    for load, store in zip(loads, stores):
        load.wait()
        store.start()
    for store in stores:
        store.wait()


def fused_kernel(
    dims,
    scale,
    fields_hbm,
    weight_hbm,
    cot_hbm,
    adjacency_ref,
    act_hbm,
    in_grad_hbm,
    w_grad_hbm,
    act_ref,
    in_grad_ref,
    w_grad_ref,
    fields_ref,
    cot_ref,
    full_w,
    edges,
    grad_edges,
    cross,
    padded,
    shifted,
    total,
    outgoing,
    from_core,
    to_x,
    from_x,
    to_z,
    from_z,
    send_sem,
    recv_sem,
    load_sem,
):
    faces, band, size, channels = dims
    cells = faces * band * size
    line = faces * size
    side = faces * 2 * band
    block = weight_hbm.shape[0]
    quarter = 4 * block
    f32, bf16 = jnp.float32, jnp.bfloat16
    me = lax.axis_index("tile")
    z = lax.axis_index("member")
    chip, core = me // 2, me % 2
    sib = chip * 2 + (1 - core)
    across = (1 - chip) * 2 + core
    diag = (1 - chip) * 2 + (1 - core)
    tile_peers = (sib, across, diag)

    def remote(src, dst, sem, target):
        return pltpu.make_async_remote_copy(
            src_ref=src,
            dst_ref=dst,
            send_sem=send_sem.at[sem],
            recv_sem=recv_sem.at[sem],
            device_id=target,
            device_id_type=MESH,
        )

    def tile_id(t):
        return {"tile": t}

    def member_id(k):
        return {"member": (z + k) % 4}

    def w_block(t, m):
        return full_w.at[pl.ds(pl.multiple_of((t * 4 + m) * block, 16), block)]

    def edge_parts(buf, first, source, target):
        top = (source == 0) | (target == source - 1)
        bottom = (source == 3) | (target == source + 1)
        spans = ((0, side, None), (side, line, top), (side + line, line, bottom))
        for part, (start, count, needed) in enumerate(spans):
            piece = buf.at[source, pl.ds(start, count)]
            yield needed, piece, first + part

    def when(needed, action):
        if needed is None:
            action()
        else:
            pl.when(needed)(action)

    def each_edge(buf, first, incoming, action):
        for k, t in enumerate(tile_peers):
            source, target = (t, me) if incoming else (me, t)
            for needed, piece, sem in edge_parts(buf, first + 3 * k, source, target):
                when(needed, functools.partial(action, remote(piece, piece, sem, tile_id(t))))

    def send_edges(buf, first):
        each_edge(buf, first, False, lambda copy: copy.start())

    def take_edges(buf, first):
        each_edge(buf, first, True, lambda copy: copy.wait_recv())

    def finish_edges(buf, first):
        each_edge(buf, first, False, lambda copy: copy.wait_send())

    load_w = pltpu.make_async_copy(weight_hbm, w_block(me, z), load_sem.at[0])
    load_fields = pltpu.make_async_copy(fields_hbm, fields_ref, load_sem.at[1])
    load_cot = pltpu.make_async_copy(cot_hbm, cot_ref, load_sem.at[2])
    for load in (load_w, load_fields, load_cot):
        load.start()

    barrier = pltpu.get_barrier_semaphore()
    for t in tile_peers:
        pl.semaphore_signal(barrier, inc=1, device_id=tile_id(t), device_id_type=MESH)
    for k in range(1, 4):
        pl.semaphore_signal(barrier, inc=1, device_id=member_id(k), device_id_type=MESH)

    row_start = me * band
    q = lane_numbers(cells)
    col, row, face = q % size, (q // size) % band, q // (size * band)
    target = face * (2 * band) + row + jnp.where(col == 0, 0, band)
    side_pick = placing(jnp.where((col == 0) | (col == size - 1), target, -1), side)

    def own_edges(values, out):
        cube = values.reshape(faces, band, size, channels)
        out[me, 0:side] = jnp.dot(side_pick, values, preferred_element_type=f32).astype(bf16)
        out[me, side : side + line] = cube[:, 0].reshape(line, channels)
        out[me, side + line : side + 2 * line] = cube[:, band - 1].reshape(line, channels)

    load_w.wait()
    pl.semaphore_wait(barrier, 6)

    started = []

    def go(copy):
        copy.start()
        started.append(copy)

    for k in (2, 1, 3):
        go(remote(w_block(me, z), w_block(me, z), WZ + k - 1, member_id(k)))
    def w_spread(k):
        part = w_block(me, (z + 4 - k) % 4)
        if k:
            remote(part, part, WZ + k - 1, member_id(k)).wait_recv()
        go(remote(part, part, WX + k, tile_id(across)))
        go(remote(part, part, WS + k, tile_id(sib)))

    w_spread(0)
    load_fields.wait()
    own_edges(fields_ref[...], edges)
    send_edges(edges, EX)

    q = lane_numbers(4 * line)
    bank, along = q // size, q % size
    base, turned = jnp.zeros_like(q), jnp.zeros_like(q)
    for f in range(faces):
        for e in range(4):
            here = bank == e * faces + f
            start = adjacency_ref[1, e, f] * line + adjacency_ref[0, e, f] * size
            base = jnp.where(here, start, base)
            turned = jnp.where(here, adjacency_ref[2, e, f], turned)
    cross[...] = placing(base + along + turned * (size - 1 - 2 * along), 4 * line)
    q = lane_numbers(4 * side)
    band_of, rest = q // side, q % side
    order = placing(
        ((rest // band) % 2) * line
        + (rest // (2 * band)) * size
        + band_of * band
        + rest % band,
        2 * line,
    )
    for k in (1, 3, 2):
        w_spread(k)

    def columns(rows):
        return lax.broadcasted_iota(jnp.int32, (rows, 1), 0) % size

    def moved(values, step):
        rows = values.shape[0]
        if step == 0:
            return values
        if step < 0:
            return jnp.where(columns(rows) == 0, 0.0, pltpu.roll(values, 1, 0))
        return jnp.where(columns(rows) == size - 1, 0.0, pltpu.roll(values, rows - 1, 0))

    def with_halo(values, buf, north, south):
        above = buf[jnp.maximum(me - 1, 0), side + line : side + 2 * line].astype(f32)
        below = buf[jnp.minimum(me + 1, 3), side : side + line].astype(f32)
        above = jnp.where(me > 0, above, north).reshape(faces, 1, size, channels)
        below = jnp.where(me < 3, below, south).reshape(faces, 1, size, channels)
        own = values.astype(f32).reshape(faces, band, size, channels)
        return jnp.concatenate([above, own, below], axis=1).reshape(-1, channels)

    def lines_of(buf):
        sides = jnp.concatenate([buf[t, 0:side] for t in range(4)], axis=0)
        sides = jnp.dot(order, sides, preferred_element_type=f32).astype(bf16)
        north = buf[0, side : side + line]
        south = buf[3, side + line : side + 2 * line]
        return jnp.concatenate([north, south, sides], axis=0)

    take_edges(edges, EX)
    cycle_cells = jnp.dot(cross[...], lines_of(edges), preferred_element_type=f32)
    center = with_halo(
        fields_ref[...], edges, cycle_cells[0:line], cycle_cells[line : 2 * line]
    )
    cycle_sides = cycle_cells[2 * line :].astype(bf16)
    q = lane_numbers(line)
    near = q % size - row_start + 1
    spot = (q // size) * ((band + 2) * size) + near * size
    inside = (near >= 0) & (near < band + 2)
    for dx in range(3):
        values = moved(center, dx - 1)
        if dx != 1:
            first = line if dx else 0
            put = placing(
                jnp.where(inside, spot + (size - 1 if dx else 0), -1), faces * (band + 2) * size
            )
            values = values + jnp.dot(
                put, cycle_sides[first : first + line], preferred_element_type=f32
            )
        padded[dx] = values.astype(bf16).reshape(faces, band + 2, size, channels)

    for k in (0, 1, 3, 2):
        part = w_block(across, (z + 4 - k) % 4)
        remote(part, part, WX + k, tile_id(across)).wait_recv()
        go(remote(part, part, WD + k, tile_id(sib)))
    for k in range(4):
        part = w_block(sib, (z + 4 - k) % 4)
        remote(part, part, WS + k, tile_id(sib)).wait_recv()
        part = w_block(diag, (z + 4 - k) % 4)
        remote(part, part, WD + k, tile_id(sib)).wait_recv()

    def window(dy, dx):
        return padded[dx, :, dy : dy + band].reshape(cells, channels)

    def w_of(dy, dx):
        first = (3 * dy + dx) * channels
        return full_w[first : first + channels]

    pre = jnp.zeros((cells, channels), f32)
    for dy in range(3):
        for dx in range(3):
            pre = pre + jnp.dot(window(dy, dx), w_of(dy, dx), preferred_element_type=f32)
    load_cot.wait()
    square = pre * pre
    bend = jnp.tanh(gelu_scale * (pre + 0.044715 * pre * square))
    act_ref[...] = (0.5 * pre * (1.0 + bend)).astype(bf16)
    keep_act = pltpu.make_async_copy(act_ref, act_hbm, load_sem.at[3])
    keep_act.start()
    slope = 0.5 * (1.0 + bend) + 0.5 * pre * (1.0 - bend * bend) * (
        gelu_scale * (1.0 + 3 * 0.044715 * square)
    )
    act_grad = (cot_ref[...].astype(f32) * slope).astype(bf16)
    own_edges(act_grad, grad_edges)

    for dy in range(3):
        for dx in range(3):
            first = (3 * dy + dx) * channels
            part = lax.dot_general(
                window(dy, dx), act_grad, (((0,), (0,)), ((), ())), preferred_element_type=f32
            )
            total[first : first + channels] = part
            outgoing[first : first + channels] = part.astype(bf16)

    def quarter_at(t):
        return pl.ds(pl.multiple_of(t * quarter, 16), quarter)

    def part_at(m):
        return pl.ds(pl.multiple_of(m * block, 16), block)

    def row_at(t, m):
        return pl.ds(pl.multiple_of((t * 4 + m) * block, 16), block)

    for k in (2, 1, 3, 0):
        m = (z + k) % 4
        there = from_core.at[0, part_at(m)]
        go(remote(outgoing.at[row_at(diag, m)], there, R1 + k, tile_id(sib)))
    go(remote(outgoing.at[quarter_at(sib)], from_core.at[1], R1 + 4, tile_id(sib)))

    for k in (2, 1, 3, 0):
        m = (z + k) % 4
        there = from_core.at[0, part_at(m)]
        remote(there, there, R1 + k, tile_id(sib)).wait_recv()
        to_x[part_at(m)] = (
            total[row_at(across, m)] + from_core[0, part_at(m)].astype(f32)
        ).astype(bf16)
        go(remote(to_x.at[part_at(m)], from_x.at[part_at(m)], X2 + k, tile_id(across)))

    send_edges(grad_edges, GX)

    remote(from_core.at[1], from_core.at[1], R1 + 4, tile_id(sib)).wait_recv()
    for k in (2, 1, 3, 0):
        m = (z + k) % 4
        remote(to_x.at[part_at(m)], from_x.at[part_at(m)], X2 + k, tile_id(across)).wait_recv()
        mine = (
            total[row_at(me, m)]
            + from_core[1, part_at(m)].astype(f32)
            + from_x[part_at(m)].astype(f32)
        )
        if k:
            to_z[k - 1] = mine.astype(bf16)
            go(remote(to_z.at[k - 1], from_z.at[k - 1], Z3 + k - 1, member_id(k)))
        else:
            w_grad_ref[...] = mine

    take_edges(grad_edges, GX)
    center = with_halo(act_grad, grad_edges, 0.0, 0.0)
    for dx in range(3):
        shifted[dx] = (
            moved(center, 1 - dx).astype(bf16).reshape(faces, band + 2, size, channels)
        )
    grad = jnp.zeros((cells, channels), f32)
    over_outputs = (((1,), (1,)), ((), ()))
    for dy in range(3):
        for dx in range(3):
            grad = grad + lax.dot_general(
                shifted[dx, :, 2 - dy : 2 - dy + band].reshape(cells, channels),
                w_of(dy, dx),
                over_outputs,
                preferred_element_type=f32,
            )

    lines = lines_of(grad_edges).astype(f32)
    taps = [moved(lines, 1 - s).astype(bf16) for s in range(3)]
    pieces = []
    for edge in range(4):
        piece = jnp.zeros((line, channels), f32)
        for s in range(3):
            dy, dx = ((0, s), (2, s), (s, 0), (s, 2))[edge]
            piece = piece + lax.dot_general(
                taps[s][edge * line : (edge + 1) * line],
                w_of(dy, dx),
                over_outputs,
                preferred_element_type=f32,
            )
        pieces.append(piece)
    cycle = jnp.concatenate(pieces, axis=0)
    high = cycle.astype(bf16)
    low = (cycle - high.astype(f32)).astype(bf16)
    q = lane_numbers(2 * line)
    lane_face, near = (q // size) % faces, q % size - row_start
    spot = lane_face * (band * size) + near * size + jnp.where(q < line, 0, size - 1)
    put = placing(jnp.where((near >= 0) & (near < band), spot, -1), cells)
    grad = grad.reshape(faces, band, size, channels)
    line_grad = jnp.zeros((4 * line, channels), f32)
    side_grad = jnp.zeros((cells, channels), f32)
    for level in (high, low):
        routed = jnp.dot(cross[...], level, preferred_element_type=f32)
        line_grad = line_grad + routed
        side_grad = side_grad + jnp.dot(
            put, routed[2 * line :].astype(bf16), preferred_element_type=f32
        )
    north = jnp.where(me == 0, line_grad[0:line], 0.0).reshape(faces, 1, size, channels)
    south = jnp.where(me == 3, line_grad[line : 2 * line], 0.0).reshape(faces, 1, size, channels)
    inner = jnp.zeros((faces, band - 2, size, channels), f32)
    grad = grad + jnp.concatenate([north, inner, south], axis=1)
    grad = grad.reshape(cells, channels) + side_grad
    in_grad_ref[...] = grad.astype(bf16)
    keep_grad = pltpu.make_async_copy(in_grad_ref, in_grad_hbm, load_sem.at[4])
    keep_grad.start()

    result = w_grad_ref[...]
    for k in range(1, 4):
        remote(from_z.at[k - 1], from_z.at[k - 1], Z3 + k - 1, member_id(k)).wait_recv()
        result = result + from_z[k - 1].astype(f32)
    w_grad_ref[...] = result * scale
    keep_w = pltpu.make_async_copy(w_grad_ref, w_grad_hbm, load_sem.at[5])
    keep_w.start()
    finish_edges(edges, EX)
    finish_edges(grad_edges, GX)
    for copy in started:
        copy.wait_send()
    keep_act.wait()
    keep_grad.wait()
    keep_w.wait()


def shards(fields, weight, cotangent, adjacency):
    members, faces, band, size, channels = fields.shape
    tiles, across = lax.axis_size("tile"), lax.axis_size("member")
    block = weight.shape[0]
    fits = tiles == 4 and across == 4 and members == 1 and band * tiles == size
    if not (fits and size == 16 and block % 16 == 0 and (faces * 2 * band) % 16 == 0):
        return plain_shards(fields, weight, cotangent, adjacency)
    cells = faces * band * size
    side, line = faces * 2 * band, faces * size
    bf16, f32 = jnp.bfloat16, jnp.float32
    scale = 1.0 / math.sqrt(cells * tiles * across)
    rows = block * tiles * across
    anywhere = pl.BlockSpec(memory_space=pl.ANY)
    results = pl.pallas_call(
        functools.partial(fused_kernel, (faces, band, size, channels), scale),
        out_shape=(
            jax.ShapeDtypeStruct((cells, channels), bf16),
            jax.ShapeDtypeStruct((cells, channels), bf16),
            jax.ShapeDtypeStruct((block, channels), f32),
        ),
        in_specs=[anywhere] * 3 + [pl.BlockSpec(memory_space=pltpu.SMEM)],
        out_specs=(anywhere,) * 3,
        scratch_shapes=[
            pltpu.VMEM((cells, channels), bf16),
            pltpu.VMEM((cells, channels), bf16),
            pltpu.VMEM((block, channels), f32),
            pltpu.VMEM((cells, channels), bf16),
            pltpu.VMEM((cells, channels), bf16),
            pltpu.VMEM((rows, channels), bf16),
            pltpu.VMEM((4, side + 2 * line, channels), bf16),
            pltpu.VMEM((4, side + 2 * line, channels), bf16),
            pltpu.VMEM((4 * line, 4 * line), bf16),
            pltpu.VMEM((3, faces, band + 2, size, channels), bf16),
            pltpu.VMEM((3, faces, band + 2, size, channels), bf16),
            pltpu.VMEM((rows, channels), f32),
            pltpu.VMEM((rows, channels), bf16),
            pltpu.VMEM((2, 4 * block, channels), bf16),
            pltpu.VMEM((4 * block, channels), bf16),
            pltpu.VMEM((4 * block, channels), bf16),
            pltpu.VMEM((3, block, channels), bf16),
            pltpu.VMEM((3, block, channels), bf16),
            pltpu.SemaphoreType.DMA((COPIES,)),
            pltpu.SemaphoreType.DMA((COPIES,)),
            pltpu.SemaphoreType.DMA((6,)),
        ],
        compiler_params=pltpu.CompilerParams(
            collective_id=0, has_side_effects=True, vmem_limit_bytes=60 * 1024 * 1024
        ),
    )(
        fields.reshape(cells, channels),
        weight,
        cotangent.reshape(cells, channels),
        adjacency.transpose(2, 1, 0),
    )
    act, in_grad, w_grad = pl.pallas_call(
        store_kernel,
        out_shape=tuple(jax.ShapeDtypeStruct(r.shape, r.dtype) for r in results),
        in_specs=[anywhere] * 3,
        out_specs=(anywhere,) * 3,
        scratch_shapes=[pltpu.VMEM(r.shape, r.dtype) for r in results]
        + [pltpu.SemaphoreType.DMA((6,))],
        compiler_params=pltpu.CompilerParams(vmem_limit_bytes=60 * 1024 * 1024),
    )(*results)
    return act.reshape(fields.shape), in_grad.reshape(fields.shape), w_grad


def solution(mesh):
    in_specs = (
        P(("groups", "member"), None, "tile", None, None),
        P(("tile", "member"), None),
        P(("groups", "member"), None, "tile", None, None),
        P(),
    )
    out_specs = (
        P(("groups", "member"), None, "tile", None, None),
        P(("groups", "member"), None, "tile", None, None),
        P(("groups", "tile", "member"), None),
    )
    return jax.shard_map(shards, mesh=mesh, in_specs=in_specs, out_specs=out_specs, check_vma=False)
```
